32 devices in a mesh: gx: 8 (over y, x, core), gy: 4 (over z).
Axes of the slice: x: 2, y: 2, z: 4, core: 2. Of those that a mesh axis runs over, the one named last changes fastest.
Arguments:
- conductance: float32 [16, 64, 512], P(None, 'gx', 'gy'), may hold values from 0.2 to 5
- labels: int32 [16, 64, 512], P(None, 'gx', 'gy'), may hold values from 0 to 2, as said below
- cotangent: float32 [2, 16, 64, 512], P(None, None, 'gx', 'gy')
- saved: float32 [2, 16, 64, 512], P(None, None, 'gx', 'gy'), may hold values from 0 to 1
Outputs:
- adjoint: float32 [2, 16, 64, 512], P(None, None, 'gx', 'gy')
- gradient: float32 [16, 64, 512], P(None, 'gx', 'gy')
The draws below stay inside these ranges and needn't reach their ends.
Inputs may be any that keep to these rules, and one draw needn't show every extreme that they name: `labels`: 0 marks an unseeded voxel, 1 or 2 the class of a seed.
All inputs are finite; a program needn't handle non-finite values.
Results may differ from the reference program's by a relative error of at most 0.0003.
Values sent between devices are 32-bit elements; how exact they have to be, the bound alone decides.
A program may use at most 64 MiB of HBM per device.

```python
import math
import jax
import jax.numpy as jnp

Z = 16
ITERS = 3
NX = 64
NY = 512


def draw_labels(key, part):
    picked = jax.random.randint(key, (Z, NX, NY), 0, 16)
    return jnp.where(picked == 0, 1, jnp.where(picked == 1, 2, 0)).astype(jnp.int32)


def draw_cotangent(key, part):
    key_base = jax.random.fold_in(key, 11)
    row_pos = jnp.arange(NX, dtype=jnp.float32) / float(max(NX - 1, 1))
    col_pos = jnp.arange(NY, dtype=jnp.float32) / float(max(NY - 1, 1))
    ramp = (1.0 + 2.0 * row_pos)[None, None, :, None] * (1.0 + col_pos)[None, None, None, :]
    base = jax.random.normal(key_base, (2, Z, NX, NY), jnp.float32)
    return (base * ramp * 0.5).astype(jnp.float32)


def steps_of(stream_key, dims, split, least, high):
    level = 1.0
    for dim, shards_of in split:
        draws = jax.random.uniform(jax.random.fold_in(jax.random.fold_in(stream_key, 6), dim), (shards_of,), jnp.float32, least / len(split), high / len(split))
        level = level * jnp.repeat(jnp.exp(draws), dims[dim] // shards_of).reshape((-1,) + (1,) * (len(dims) - 1 - dim))
    return level


def setup_inputs(seed: int = 0) -> dict:
    key_of = jax.random.split(jax.random.key(seed), 5)
    return {
        "conductance": jnp.clip(jnp.exp(math.log(5.0) - 3.218876 * jax.random.uniform(key_of[0], (Z, NX, NY), jnp.float32) ** steps_of(key_of[0], (Z, NX, NY), ((1, 8), (2, 4)), -0.2, 0.2)), 0.2, 5.0),
        "labels": draw_labels(jax.random.fold_in(key_of[4], 71), 0),
        "cotangent": draw_cotangent(jax.random.fold_in(key_of[4], 71), 0),
        "saved": jnp.clip(1.0 * jax.random.uniform(key_of[3], (2, Z, NX, NY), jnp.float32) ** steps_of(key_of[3], (2, Z, NX, NY), ((2, 8), (3, 4)), -0.2, 0.2), 0.0, 1.0),
    }


prior_strength = 1.0


def potentials(labels, saved):
    classes = jnp.arange(1, 3, dtype=jnp.int32)[:, None, None, None]
    tagged = labels[None]
    return jnp.where(tagged == classes, 1.0, jnp.where(tagged > 0, 0.0, saved)).astype(jnp.float32)


def edge_weights(conductance):
    edge_x = 0.5 * (conductance[:, :-1, :] + conductance[:, 1:, :])
    edge_y = 0.5 * (conductance[:, :, :-1] + conductance[:, :, 1:])
    edge_z = 0.5 * (conductance[:-1] + conductance[1:])
    return edge_x, edge_y, edge_z


def pad_after(fluxes, axis_num):
    widths = [(0, 0)] * fluxes.ndim
    widths[axis_num] = (0, 1)
    return jnp.pad(fluxes, widths)


def pad_before(fluxes, axis_num):
    widths = [(0, 0)] * fluxes.ndim
    widths[axis_num] = (1, 0)
    return jnp.pad(fluxes, widths)


def apply_graph_laplacian(input_vector, weight_field):
    edge_x, edge_y, edge_z = weight_field
    flux_x = edge_x * (-jnp.diff(input_vector, axis=2))
    flux_y = edge_y * (-jnp.diff(input_vector, axis=3))
    flux_z = edge_z * (-jnp.diff(input_vector, axis=1))
    total = pad_after(flux_x, 2) - pad_before(flux_x, 2)
    total = total + pad_after(flux_y, 3) - pad_before(flux_y, 3)
    total = total + pad_after(flux_z, 1) - pad_before(flux_z, 1)
    return total


def apply_operator(input_vector, unlabelled_mask, weight_field):
    mask_applied = unlabelled_mask * input_vector
    return unlabelled_mask * (prior_strength * mask_applied + apply_graph_laplacian(mask_applied, weight_field)) + (1.0 - unlabelled_mask) * input_vector


def edge_gradient(adjoint, potential, axis_num):
    return -jnp.sum(jnp.diff(adjoint, axis=axis_num) * jnp.diff(potential, axis=axis_num), axis=0)


def reference(conductance, labels, cotangent, saved):
    weight_field = edge_weights(conductance)
    unlabelled_mask = (labels == 0).astype(jnp.float32)[None]
    solver_residual = unlabelled_mask * cotangent
    search_direction = solver_residual
    adjoint = jnp.zeros_like(solver_residual)
    norm_now = jnp.sum(solver_residual * solver_residual, axis=(1, 2, 3))
    for iteration in range(ITERS):
        operator_result = apply_operator(search_direction, unlabelled_mask, weight_field)
        step_size = norm_now / jnp.sum(search_direction * operator_result, axis=(1, 2, 3))
        adjoint = adjoint + step_size[:, None, None, None] * search_direction
        solver_residual = solver_residual - step_size[:, None, None, None] * operator_result
        if iteration + 1 < ITERS:
            norm_next = jnp.sum(solver_residual * solver_residual, axis=(1, 2, 3))
            search_direction = solver_residual + (norm_next / norm_now)[:, None, None, None] * search_direction
            norm_now = norm_next
    potential = potentials(labels, saved)
    grad_x = edge_gradient(adjoint, potential, 2)
    grad_y = edge_gradient(adjoint, potential, 3)
    grad_z = edge_gradient(adjoint, potential, 1)
    total = pad_after(grad_x, 1) + pad_before(grad_x, 1)
    total = total + pad_after(grad_y, 2) + pad_before(grad_y, 2)
    total = total + pad_after(grad_z, 0) + pad_before(grad_z, 0)
    return adjoint, 0.5 * total
```

```python
import jax
import jax.numpy as jnp
from jax import lax
from jax.experimental import pallas as pl
from jax.experimental.pallas import tpu as pltpu
from jax.sharding import PartitionSpec as P

SHIFT = 2.0
SCALE = 32.0
HALO = 3
MESH = pl.DeviceIdType.MESH


def kernel(
    n_gx, n_gy,
    cond_ref, label_ref, cot_ref, saved_ref,
    adj_ref, grad_ref,
    ce, me, pe, v0, v1, v2, wx, wy, wz, dd, gk,
    xsend, xrecv, ysend, yrecv, pay, slots_x, mid, slots_y,
    send_sem, recv_sem, gx_send, gx_recv, gy_send, gy_recv,
):
    depth, rows, cols = cond_ref.shape
    R2, C2 = 2 * rows, 2 * cols
    gx = lax.axis_index("gx")
    gy = lax.axis_index("gy")
    has_up, has_down = gx > 0, gx < n_gx - 1
    has_left, has_right = gy > 0, gy < n_gy - 1

    sides = [(-1, 0), (1, 0), (0, -1), (0, 1), (-1, -1), (-1, 1), (1, -1), (1, 1)]

    def exists(dx, dy):
        ok = None
        for d, low, high in ((dx, has_up, has_down), (dy, has_left, has_right)):
            if d:
                here = low if d < 0 else high
                ok = here if ok is None else jnp.logical_and(ok, here)
        return ok

    barrier = pltpu.get_barrier_semaphore()
    for o in range(1, n_gx):
        pl.semaphore_signal(barrier, inc=1, device_id=(lax.rem(gx + o, n_gx), gy), device_id_type=MESH)
    for o in range(1, n_gy):
        pl.semaphore_signal(barrier, inc=1, device_id=(gx, lax.rem(gy + o, n_gy)), device_id_type=MESH)
    for dx, dy in sides[4:]:
        @pl.when(exists(dx, dy))
        def _():
            pl.semaphore_signal(barrier, inc=1, device_id=(gx + dx, gy + dy), device_id_type=MESH)

    lane = lax.broadcasted_iota(jnp.int32, (rows, cols), 1)
    slot_lanes = cols // depth
    packs = [jnp.zeros((rows, cols), jnp.float32) for _ in range(6)]
    zero_tile = jnp.zeros((rows, cols), jnp.float32)
    for z in range(depth):
        lab = label_ref[z]
        m = jnp.where(lab == 0, 1.0, 0.0)
        fields = [m * cot_ref[0, z], m * cot_ref[1, z], cond_ref[z], m]
        for k in range(2):
            fields.append(jnp.where(lab == k + 1, 1.0, jnp.where(lab > 0, 0.0, saved_ref[k, z])))
        v0[0, z + 1, 0:rows, 0:cols] = fields[0]
        v0[1, z + 1, 0:rows, 0:cols] = fields[1]
        ce[z, 0:rows, 0:cols] = fields[2]
        me[z, 0:rows, 0:cols] = m
        pe[0, z, 0:rows, 0:cols] = fields[4]
        pe[1, z, 0:rows, 0:cols] = fields[5]
        at = 0
        for f, width in zip(fields, (3, 3, 3, 2, 1, 1)):
            first = at + z * width
            xsend[0, first:first + width, :] = f[0:width]
            xsend[1, first:first + width, :] = f[rows - width:rows]
            at += depth * width
        window = lax.rem(lane - z * slot_lanes + HALO + cols, cols) < 2 * HALO
        for i, f in enumerate(fields):
            rolled = pltpu.roll(f, z * slot_lanes, 1) if z else f
            packs[i] = jnp.where(window, rolled, packs[i])
    for i in range(6):
        ysend[i] = packs[i]

    partners = n_gx - 1 + n_gy - 1
    for dx, dy in sides[4:]:
        partners = partners + jnp.where(exists(dx, dy), 1, 0)
    pl.semaphore_wait(barrier, partners)

    def halo_copy(i):
        dx, dy = sides[i]
        back = sides.index((-dx, -dy))
        if dy == 0:
            src, dst = xsend.at[0 if dx < 0 else 1], xrecv.at[back]
        else:
            src, dst = ysend, yrecv.at[back - 2]
        return pltpu.make_async_remote_copy(
            src_ref=src, dst_ref=dst, send_sem=send_sem.at[i], recv_sem=recv_sem.at[back],
            device_id=(gx + dx, gy + dy), device_id_type=MESH,
        )

    def arrival(i):
        dst = xrecv.at[i] if i < 2 else yrecv.at[i - 2]
        return pltpu.make_async_remote_copy(
            src_ref=dst, dst_ref=dst, send_sem=send_sem.at[i], recv_sem=recv_sem.at[i],
            device_id=(gx + sides[i][0], gy + sides[i][1]), device_id_type=MESH,
        )

    for i, (dx, dy) in enumerate(sides):
        @pl.when(exists(dx, dy))
        def _():
            halo_copy(i).start()

        @pl.when(jnp.logical_not(exists(dx, dy)))
        def _():
            if i < 2:
                xrecv[i] = jnp.zeros(xrecv.shape[1:], jnp.float32)
            else:
                yrecv[i - 2] = jnp.zeros(yrecv.shape[1:], jnp.float32)

    edge = jnp.zeros((R2, C2), jnp.float32)
    for v in (v0, v1, v2):
        for k in range(2):
            v[k, 0] = edge
            v[k, depth + 1] = edge
    wz[0] = edge
    for z in range(depth):
        for ref in (v0.at[0, z + 1], v0.at[1, z + 1], ce.at[z], me.at[z], pe.at[0, z], pe.at[1, z]):
            ref[rows:R2, 0:cols] = zero_tile

    for i, (dx, dy) in enumerate(sides):
        @pl.when(exists(dx, dy))
        def _():
            arrival(i).wait_recv()

    row = lax.broadcasted_iota(jnp.int32, (rows, cols), 0)
    after = lax.rem(lane, slot_lanes) < HALO
    beside, corner = [], []
    for i in range(6):
        beside.append(jnp.where(after, yrecv[1, i], yrecv[0, i]))
        if i < 4:
            above = jnp.where(after, yrecv[3, i], yrecv[2, i])
            below = jnp.where(after, yrecv[5, i], yrecv[4, i])
            corner.append(jnp.where(row < rows // 2, below, above))
    window = jnp.logical_or(lane < HALO, lane >= cols - HALO)
    corner_rows = jnp.logical_or(row < HALO, row >= rows - HALO)
    window_corner = jnp.logical_and(window, corner_rows)
    for z in range(depth):
        targets = [v0.at[0, z + 1], v0.at[1, z + 1], ce.at[z], me.at[z], pe.at[0, z], pe.at[1, z]]
        at = 0
        for f, (ref, width) in enumerate(zip(targets, (3, 3, 3, 2, 1, 1))):
            first = at + z * width
            ref[rows:rows + width, 0:cols] = xrecv[1, first:first + width, :]
            ref[R2 - width:R2, 0:cols] = xrecv[0, first:first + width, :]
            at += depth * width
            back = (cols - z * slot_lanes) % cols
            tile = pltpu.roll(beside[f], back, 1) if back else beside[f]
            ref[0:rows, cols:C2] = jnp.where(window, tile, 0.0)
            if f < 4:
                tile = pltpu.roll(corner[f], back, 1) if back else corner[f]
                ref[rows:R2, cols:C2] = jnp.where(window_corner, tile, 0.0)

    big_row = lax.broadcasted_iota(jnp.int32, (R2, C2), 0)
    big_lane = lax.broadcasted_iota(jnp.int32, (R2, C2), 1)
    no_x = jnp.logical_or(
        jnp.logical_and(big_row == rows - 1, jnp.logical_not(has_down)),
        jnp.logical_and(big_row == R2 - 1, jnp.logical_not(has_up)),
    )
    no_y = jnp.logical_or(
        jnp.logical_and(big_lane == cols - 1, jnp.logical_not(has_right)),
        jnp.logical_and(big_lane == C2 - 1, jnp.logical_not(has_left)),
    )
    valid_x = jnp.where(no_x, 0.0, 1.0)
    valid_y = jnp.where(no_y, 0.0, 1.0)
    half_x = valid_x * (0.5 / SCALE)
    half_y = valid_y * (0.5 / SCALE)
    last = depth - 1

    def next_row(a):
        return pltpu.roll(a, a.shape[0] - 1, 0)

    def next_lane(a):
        return pltpu.roll(a, a.shape[1] - 1, 1)

    def weights(z, carry):
        c = ce[z]
        ex = half_x * (c + next_row(c))
        ey = half_y * (c + next_lane(c))
        cn = ce[jnp.minimum(z + 1, last)]
        ez = jnp.where(z < last, 0.5 / SCALE, 0.0) * (c + cn)
        wx[z] = ex
        wy[z] = ey
        wz[z + 1] = ez
        deg = ex + pltpu.roll(ex, 1, 0) + ey + pltpu.roll(ey, 1, 1) + ez + wz[z]
        dd[z] = deg + (1.0 - SHIFT) / SCALE
        return carry

    lax.fori_loop(0, depth, weights, 0, unroll=2)

    def apply_full(src, dst, sums):
        def body(z, carry):
            ex, ey, ez, ezm, d, m = wx[z], wy[z], wz[z + 1], wz[z], dd[z], me[z]
            out = []
            for k in range(2):
                v = src[k, z + 1]
                a = d * v - ez * src[k, z + 2] - ezm * src[k, z]
                a = a - ex * next_row(v) - pltpu.roll(ex * v, 1, 0)
                a = a - ey * next_lane(v) - pltpu.roll(ey * v, 1, 1)
                a = m * a
                dst[k, z + 1] = a
                old, new = v[0:rows, 0:cols], a[0:rows, 0:cols]
                out.append(carry[3 * k] + old * old)
                out.append(carry[3 * k + 1] + old * new)
                out.append(carry[3 * k + 2] + new * new)
            return tuple(out)
        return lax.fori_loop(0, depth, body, (zero_tile,) * 6, unroll=2)

    first = apply_full(v0, v1, True)
    second = apply_full(v1, v2, True)

    def apply_core(z, carry):
        exr = wx[z, :, 0:cols]
        eyr = wy[z, 0:rows, :]
        ez, ezm = wz[z + 1, 0:rows, 0:cols], wz[z, 0:rows, 0:cols]
        d, m = dd[z, 0:rows, 0:cols], me[z, 0:rows, 0:cols]
        out = []
        for k in range(2):
            vx = v2[k, z + 1, :, 0:cols]
            vy = v2[k, z + 1, 0:rows, :]
            v = vx[0:rows]
            a = d * v - ez * v2[k, z + 2, 0:rows, 0:cols] - ezm * v2[k, z, 0:rows, 0:cols]
            a = a - (exr * next_row(vx) + pltpu.roll(exr * vx, 1, 0))[0:rows]
            a = a - (eyr * next_lane(vy) + pltpu.roll(eyr * vy, 1, 1))[:, 0:cols]
            out.append(carry[k] + v * (m * a))
        return tuple(out)

    third = lax.fori_loop(0, depth, apply_core, (zero_tile,) * 2, unroll=2)

    for k in range(2):
        moments = [first[3 * k], first[3 * k + 1], first[3 * k + 2],
                   second[3 * k + 1], second[3 * k + 2], third[k]]
        for j, a in enumerate(moments):
            pay[8 * k + j:8 * k + j + 1, :] = jnp.sum(a, axis=0, keepdims=True)
        pay[8 * k + 6:8 * k + 8, :] = jnp.zeros((2, cols), jnp.float32)

    def gx_copy(o):
        return pltpu.make_async_remote_copy(
            src_ref=pay, dst_ref=slots_x.at[gx], send_sem=gx_send.at[o], recv_sem=gx_recv.at[o],
            device_id=(lax.rem(gx + o, n_gx), gy), device_id_type=MESH,
        )

    def gy_copy(o):
        return pltpu.make_async_remote_copy(
            src_ref=mid, dst_ref=slots_y.at[gy], send_sem=gy_send.at[o], recv_sem=gy_recv.at[o],
            device_id=(gx, lax.rem(gy + o, n_gy)), device_id_type=MESH,
        )

    for o in range(1, n_gx):
        gx_copy(o).start()
    slots_x[gx] = pay[...]

    vx_edge = valid_x[:, 0:cols]
    vy_edge = valid_y[0:rows, :]

    def parts(k):
        def body(z, carry):
            up = jnp.minimum(z + 1, last)
            down = jnp.maximum(z - 1, 0)
            px = pe[k, z, :, 0:cols]
            py = pe[k, z, 0:rows, :]
            p = px[0:rows]
            dx = vx_edge * (px - next_row(px))
            dy = vy_edge * (py - next_lane(py))
            du = p - pe[k, up, 0:rows, 0:cols]
            dn = p - pe[k, down, 0:rows, 0:cols]
            for j, v in enumerate((v0, v1, v2)):
                ax = v[k, z + 1, :, 0:cols]
                ay = v[k, z + 1, 0:rows, :]
                a = ax[0:rows]
                qx = dx * (ax - next_row(ax))
                qy = dy * (ay - next_lane(ay))
                g = qx[0:rows] + pltpu.roll(qx, 1, 0)[0:rows]
                g = g + qy[:, 0:cols] + pltpu.roll(qy, 1, 1)[:, 0:cols]
                g = g + du * (a - v[k, z + 2, 0:rows, 0:cols])
                g = g + dn * (a - v[k, z, 0:rows, 0:cols])
                gk[3 * k + j, z] = g
            return carry
        lax.fori_loop(0, depth, body, 0, unroll=2)

    parts(0)
    for o in range(1, n_gx):
        gx_copy(o).wait_recv()
    total = slots_x[0]
    for i in range(1, n_gx):
        total = total + slots_x[i]
    mid[...] = total
    for o in range(1, n_gy):
        gy_copy(o).start()
    slots_y[gy] = total
    parts(1)
    for o in range(1, n_gy):
        gy_copy(o).wait_recv()
    total = slots_y[0]
    for i in range(1, n_gy):
        total = total + slots_y[i]
    total = jnp.broadcast_to(jnp.sum(total, axis=1, keepdims=True), total.shape)

    coeffs = []
    for k in range(2):
        m = [total[8 * k + j:8 * k + j + 1, :] for j in range(6)]
        h = [SCALE * m[j + 1] + SHIFT * m[j] for j in range(5)]
        l1, l2 = h[1] / h[0], h[2] / h[0]
        a11, a12, a22 = h[2] - l1 * h[1], h[3] - l1 * h[2], h[4] - l2 * h[2]
        b1, b2 = m[1] - l1 * m[0], m[2] - l2 * m[0]
        l3 = a12 / a11
        c2 = (b2 - l3 * b1) / (a22 - l3 * a12)
        c1 = (b1 - a12 * c2) / a11
        c0 = (m[0] - h[1] * c1 - h[2] * c2) / h[0]
        coeffs.append([jnp.broadcast_to(c, (rows, cols)) for c in (c0, c1, c2)])

    for z in range(depth):
        grad = zero_tile
        for k in range(2):
            acc = zero_tile
            for j, v in enumerate((v0, v1, v2)):
                acc = acc + coeffs[k][j] * v[k, z + 1, 0:rows, 0:cols]
                grad = grad + coeffs[k][j] * gk[3 * k + j, z]
            adj_ref[k, z] = acc
        grad_ref[z] = -0.5 * grad

    for i, (dx, dy) in enumerate(sides):
        @pl.when(exists(dx, dy))
        def _():
            halo_copy(i).wait_send()
    for o in range(1, n_gx):
        gx_copy(o).wait_send()
    for o in range(1, n_gy):
        gy_copy(o).wait_send()


def solution(mesh):
    n_gx, n_gy = mesh.shape["gx"], mesh.shape["gy"]

    def per_device(conductance, labels, cotangent, saved):
        depth, rows, cols = conductance.shape
        f32 = jnp.float32
        big = (depth, 2 * rows, 2 * cols)
        padded = (2, depth + 2, 2 * rows, 2 * cols)
        face = depth * 13
        vmem = pl.BlockSpec(memory_space=pltpu.VMEM)
        dma = pltpu.SemaphoreType.DMA
        return pl.pallas_call(
            lambda *refs: kernel(n_gx, n_gy, *refs),
            out_shape=(
                jax.ShapeDtypeStruct(cotangent.shape, f32),
                jax.ShapeDtypeStruct(conductance.shape, f32),
            ),
            in_specs=[vmem] * 4,
            out_specs=(vmem, vmem),
            scratch_shapes=[
                pltpu.VMEM(big, f32),
                pltpu.VMEM(big, f32),
                pltpu.VMEM((2,) + big, f32),
                pltpu.VMEM(padded, f32),
                pltpu.VMEM(padded, f32),
                pltpu.VMEM(padded, f32),
                pltpu.VMEM(big, f32),
                pltpu.VMEM(big, f32),
                pltpu.VMEM((depth + 1, 2 * rows, 2 * cols), f32),
                pltpu.VMEM(big, f32),
                pltpu.VMEM((6, depth, rows, cols), f32),
                pltpu.VMEM((2, face, cols), f32),
                pltpu.VMEM((2, face, cols), f32),
                pltpu.VMEM((6, rows, cols), f32),
                pltpu.VMEM((6, 6, rows, cols), f32),
                pltpu.VMEM((16, cols), f32),
                pltpu.VMEM((n_gx, 16, cols), f32),
                pltpu.VMEM((16, cols), f32),
                pltpu.VMEM((n_gy, 16, cols), f32),
                dma((8,)),
                dma((8,)),
                dma((n_gx,)),
                dma((n_gx,)),
                dma((n_gy,)),
                dma((n_gy,)),
            ],
            compiler_params=pltpu.CompilerParams(
                collective_id=0, has_side_effects=True, vmem_limit_bytes=32 * 1024 * 1024
            ),
        )(conductance, labels, cotangent, saved)

    return jax.shard_map(
        per_device,
        mesh=mesh,
        in_specs=(
            P(None, "gx", "gy"),
            P(None, "gx", "gy"),
            P(None, None, "gx", "gy"),
            P(None, None, "gx", "gy"),
        ),
        out_specs=(P(None, None, "gx", "gy"), P(None, "gx", "gy")),
        check_vma=False,
    )
```

```python
import jax
import jax.numpy as jnp
from jax import lax
from jax.experimental import pallas as pl
from jax.experimental.pallas import tpu as pltpu
from jax.sharding import PartitionSpec as P

SHIFT = 2.0
SCALE = 32.0
HALO = 3
MESH = pl.DeviceIdType.MESH


def kernel(
    n_gx, n_gy,
    cond_hbm, label_hbm, cot_hbm, saved_hbm,
    adj_ref, grad_ref,
    cond_ref, label_ref, cot_ref, saved_ref, in_sem,
    ce, me, pe, v0, v1, v2, wx, wy, wz, dd, gk,
    xsend, xrecv, ysend, yrecv, table, pay, slots_x, mid, slots_y,
    send_sem, recv_sem, gx_send, gx_recv, gy_send, gy_recv,
):
    depth, rows, cols = cond_ref.shape
    R2, C2 = 2 * rows, 2 * cols
    gx = lax.axis_index("gx")
    gy = lax.axis_index("gy")
    has_up, has_down = gx > 0, gx < n_gx - 1
    has_left, has_right = gy > 0, gy < n_gy - 1

    sides = [(-1, 0), (1, 0), (0, -1), (0, 1), (-1, -1), (-1, 1), (1, -1), (1, 1)]

    def exists(dx, dy):
        ok = None
        for d, low, high in ((dx, has_up, has_down), (dy, has_left, has_right)):
            if d:
                here = low if d < 0 else high
                ok = here if ok is None else jnp.logical_and(ok, here)
        return ok

    fetches = [
        pltpu.make_async_copy(src, dst, in_sem.at[i])
        for i, (src, dst) in enumerate((
            (cond_hbm, cond_ref), (label_hbm, label_ref), (cot_hbm, cot_ref), (saved_hbm, saved_ref),
        ))
    ]
    for fetch in fetches:
        fetch.start()

    barrier = pltpu.get_barrier_semaphore()
    for o in range(1, n_gx):
        pl.semaphore_signal(barrier, inc=1, device_id=(lax.rem(gx + o, n_gx), gy), device_id_type=MESH)
    for o in range(1, n_gy):
        pl.semaphore_signal(barrier, inc=1, device_id=(gx, lax.rem(gy + o, n_gy)), device_id_type=MESH)
    for dx, dy in sides[4:]:
        @pl.when(exists(dx, dy))
        def _():
            pl.semaphore_signal(barrier, inc=1, device_id=(gx + dx, gy + dy), device_id_type=MESH)

    zero_tile = jnp.zeros((rows, cols), jnp.float32)

    edge = jnp.zeros((R2, C2), jnp.float32)
    for v in (v0, v1, v2):
        for k in range(2):
            v[k, 0] = edge
            v[k, depth + 1] = edge
    wz[0] = edge
    for z in range(depth):
        for ref in (v0.at[0, z + 1], v0.at[1, z + 1], ce.at[z], me.at[z], pe.at[0, z], pe.at[1, z]):
            ref[rows:R2, 0:cols] = zero_tile
    for i, (dx, dy) in enumerate(sides):
        @pl.when(jnp.logical_not(exists(dx, dy)))
        def _():
            if i < 2:
                xrecv[i] = jnp.zeros(xrecv.shape[1:], jnp.float32)
            else:
                yrecv[i - 2] = jnp.zeros(yrecv.shape[1:], jnp.float32)

    for fetch in fetches:
        fetch.wait()

    lane = lax.broadcasted_iota(jnp.int32, (rows, cols), 1)
    slot_lanes = cols // depth
    packs = [jnp.zeros((rows, cols), jnp.float32) for _ in range(6)]
    for z in range(depth):
        lab = label_ref[z]
        m = jnp.where(lab == 0, 1.0, 0.0)
        fields = [m * cot_ref[0, z], m * cot_ref[1, z], cond_ref[z], m]
        for k in range(2):
            fields.append(jnp.where(lab == k + 1, 1.0, jnp.where(lab > 0, 0.0, saved_ref[k, z])))
        v0[0, z + 1, 0:rows, 0:cols] = fields[0]
        v0[1, z + 1, 0:rows, 0:cols] = fields[1]
        ce[z, 0:rows, 0:cols] = fields[2]
        me[z, 0:rows, 0:cols] = m
        pe[0, z, 0:rows, 0:cols] = fields[4]
        pe[1, z, 0:rows, 0:cols] = fields[5]
        at = 0
        for f, width in zip(fields, (3, 3, 3, 2, 1, 1)):
            first = at + z * width
            xsend[0, first:first + width, :] = f[0:width]
            xsend[1, first:first + width, :] = f[rows - width:rows]
            at += depth * width
        window = lax.rem(lane - z * slot_lanes + HALO + cols, cols) < 2 * HALO
        for i, f in enumerate(fields):
            rolled = pltpu.roll(f, z * slot_lanes, 1) if z else f
            packs[i] = jnp.where(window, rolled, packs[i])
    for i in range(6):
        ysend[i] = packs[i]

    partners = n_gx - 1 + n_gy - 1
    for dx, dy in sides[4:]:
        partners = partners + jnp.where(exists(dx, dy), 1, 0)
    pl.semaphore_wait(barrier, partners)

    def halo_copy(i):
        dx, dy = sides[i]
        back = sides.index((-dx, -dy))
        if dy == 0:
            src, dst = xsend.at[0 if dx < 0 else 1], xrecv.at[back]
        else:
            src, dst = ysend, yrecv.at[back - 2]
        return pltpu.make_async_remote_copy(
            src_ref=src, dst_ref=dst, send_sem=send_sem.at[i], recv_sem=recv_sem.at[back],
            device_id=(gx + dx, gy + dy), device_id_type=MESH,
        )

    def arrival(i):
        dst = xrecv.at[i] if i < 2 else yrecv.at[i - 2]
        return pltpu.make_async_remote_copy(
            src_ref=dst, dst_ref=dst, send_sem=send_sem.at[i], recv_sem=recv_sem.at[i],
            device_id=(gx + sides[i][0], gy + sides[i][1]), device_id_type=MESH,
        )

    for i, (dx, dy) in enumerate(sides):
        @pl.when(exists(dx, dy))
        def _():
            halo_copy(i).start()

    for i, (dx, dy) in enumerate(sides[2:], 2):
        @pl.when(exists(dx, dy))
        def _():
            arrival(i).wait_recv()

    row = lax.broadcasted_iota(jnp.int32, (rows, cols), 0)
    after = lax.rem(lane, slot_lanes) < HALO
    beside, corner = [], []
    for i in range(6):
        beside.append(jnp.where(after, yrecv[1, i], yrecv[0, i]))
        if i < 4:
            above = jnp.where(after, yrecv[3, i], yrecv[2, i])
            below = jnp.where(after, yrecv[5, i], yrecv[4, i])
            corner.append(jnp.where(row < rows // 2, below, above))
    window = jnp.logical_or(lane < HALO, lane >= cols - HALO)
    corner_rows = jnp.logical_or(row < HALO, row >= rows - HALO)
    window_corner = jnp.logical_and(window, corner_rows)
    def targets(z):
        return [v0.at[0, z + 1], v0.at[1, z + 1], ce.at[z], me.at[z], pe.at[0, z], pe.at[1, z]]

    for z in range(depth):
        for f, ref in enumerate(targets(z)):
            back = (cols - z * slot_lanes) % cols
            tile = pltpu.roll(beside[f], back, 1) if back else beside[f]
            ref[0:rows, cols:C2] = jnp.where(window, tile, 0.0)
            if f < 4:
                tile = pltpu.roll(corner[f], back, 1) if back else corner[f]
                ref[rows:R2, cols:C2] = jnp.where(window_corner, tile, 0.0)

    for i, (dx, dy) in enumerate(sides[:2]):
        @pl.when(exists(dx, dy))
        def _():
            arrival(i).wait_recv()

    for z in range(depth):
        at = 0
        for ref, width in zip(targets(z), (3, 3, 3, 2, 1, 1)):
            first = at + z * width
            ref[rows:rows + width, 0:cols] = xrecv[1, first:first + width, :]
            ref[R2 - width:R2, 0:cols] = xrecv[0, first:first + width, :]
            at += depth * width

    big_row = lax.broadcasted_iota(jnp.int32, (R2, C2), 0)
    big_lane = lax.broadcasted_iota(jnp.int32, (R2, C2), 1)
    no_x = jnp.logical_or(
        jnp.logical_and(big_row == rows - 1, jnp.logical_not(has_down)),
        jnp.logical_and(big_row == R2 - 1, jnp.logical_not(has_up)),
    )
    no_y = jnp.logical_or(
        jnp.logical_and(big_lane == cols - 1, jnp.logical_not(has_right)),
        jnp.logical_and(big_lane == C2 - 1, jnp.logical_not(has_left)),
    )
    valid_x = jnp.where(no_x, 0.0, 1.0)
    valid_y = jnp.where(no_y, 0.0, 1.0)
    half_x = valid_x * (0.5 / SCALE)
    half_y = valid_y * (0.5 / SCALE)
    last = depth - 1

    def next_row(a):
        return pltpu.roll(a, a.shape[0] - 1, 0)

    def next_lane(a):
        return pltpu.roll(a, a.shape[1] - 1, 1)

    def weights(z, carry):
        c = ce[z]
        ex = half_x * (c + next_row(c))
        ey = half_y * (c + next_lane(c))
        cn = ce[jnp.minimum(z + 1, last)]
        ez = jnp.where(z < last, 0.5 / SCALE, 0.0) * (c + cn)
        wx[z] = ex
        wy[z] = ey
        wz[z + 1] = ez
        deg = ex + pltpu.roll(ex, 1, 0) + ey + pltpu.roll(ey, 1, 1) + ez + wz[z]
        dd[z] = deg + (1.0 - SHIFT) / SCALE
        return carry

    lax.fori_loop(0, depth, weights, 0, unroll=depth)

    def apply_full(src, dst, sums):
        def body(z, carry):
            ex, ey, ez, ezm, d, m = wx[z], wy[z], wz[z + 1], wz[z], dd[z], me[z]
            out = []
            for k in range(2):
                v = src[k, z + 1]
                a = d * v - ez * src[k, z + 2] - ezm * src[k, z]
                a = a - ex * next_row(v) - pltpu.roll(ex * v, 1, 0)
                a = a - ey * next_lane(v) - pltpu.roll(ey * v, 1, 1)
                a = m * a
                dst[k, z + 1] = a
                old, new = v[0:rows, 0:cols], a[0:rows, 0:cols]
                out.append(carry[3 * k] + old * old)
                out.append(carry[3 * k + 1] + old * new)
                out.append(carry[3 * k + 2] + new * new)
            return tuple(out)
        return lax.fori_loop(0, depth, body, (zero_tile,) * 6, unroll=depth)

    first = apply_full(v0, v1, True)
    second = apply_full(v1, v2, True)

    def apply_core(z, carry):
        exr = wx[z, :, 0:cols]
        eyr = wy[z, 0:rows, :]
        ez, ezm = wz[z + 1, 0:rows, 0:cols], wz[z, 0:rows, 0:cols]
        d, m = dd[z, 0:rows, 0:cols], me[z, 0:rows, 0:cols]
        out = []
        for k in range(2):
            vx = v2[k, z + 1, :, 0:cols]
            vy = v2[k, z + 1, 0:rows, :]
            v = vx[0:rows]
            a = d * v - ez * v2[k, z + 2, 0:rows, 0:cols] - ezm * v2[k, z, 0:rows, 0:cols]
            a = a - (exr * next_row(vx) + pltpu.roll(exr * vx, 1, 0))[0:rows]
            a = a - (eyr * next_lane(vy) + pltpu.roll(eyr * vy, 1, 1))[:, 0:cols]
            out.append(carry[k] + v * (m * a))
        return tuple(out)

    third = lax.fori_loop(0, depth, apply_core, (zero_tile,) * 2, unroll=depth)

    for k in range(2):
        moments = [first[3 * k], first[3 * k + 1], first[3 * k + 2],
                   second[3 * k + 1], second[3 * k + 2], third[k]]
        for j, a in enumerate(moments):
            table[8 * k + j:8 * k + j + 1, :] = jnp.sum(a, axis=0, keepdims=True)
        table[8 * k + 6:8 * k + 8, :] = jnp.zeros((2, cols), jnp.float32)
    diagonal = lax.broadcasted_iota(jnp.int32, (16, cols), 0) == lax.broadcasted_iota(jnp.int32, (16, cols), 1)
    sums = jnp.broadcast_to(jnp.sum(table[...], axis=1, keepdims=True), (16, cols))
    pay[...] = jnp.sum(jnp.where(diagonal, sums, 0.0), axis=0, keepdims=True)

    def gx_copy(o):
        return pltpu.make_async_remote_copy(
            src_ref=pay, dst_ref=slots_x.at[gx], send_sem=gx_send.at[o], recv_sem=gx_recv.at[o],
            device_id=(lax.rem(gx + o, n_gx), gy), device_id_type=MESH,
        )

    def gy_copy(o):
        return pltpu.make_async_remote_copy(
            src_ref=mid, dst_ref=slots_y.at[gy], send_sem=gy_send.at[o], recv_sem=gy_recv.at[o],
            device_id=(gx, lax.rem(gy + o, n_gy)), device_id_type=MESH,
        )

    for o in range(1, n_gx):
        gx_copy(o).start()
    slots_x[gx] = pay[...]

    vx_edge = valid_x[:, 0:cols]
    vy_edge = valid_y[0:rows, :]

    def parts(k):
        def body(z, carry):
            up = jnp.minimum(z + 1, last)
            down = jnp.maximum(z - 1, 0)
            px = pe[k, z, :, 0:cols]
            py = pe[k, z, 0:rows, :]
            p = px[0:rows]
            dx = vx_edge * (px - next_row(px))
            dy = vy_edge * (py - next_lane(py))
            du = p - pe[k, up, 0:rows, 0:cols]
            dn = p - pe[k, down, 0:rows, 0:cols]
            for j, v in enumerate((v0, v1, v2)):
                ax = v[k, z + 1, :, 0:cols]
                ay = v[k, z + 1, 0:rows, :]
                a = ax[0:rows]
                qx = dx * (ax - next_row(ax))
                qy = dy * (ay - next_lane(ay))
                g = qx[0:rows] + pltpu.roll(qx, 1, 0)[0:rows]
                g = g + qy[:, 0:cols] + pltpu.roll(qy, 1, 1)[:, 0:cols]
                g = g + du * (a - v[k, z + 2, 0:rows, 0:cols])
                g = g + dn * (a - v[k, z, 0:rows, 0:cols])
                gk[3 * k + j, z] = g
            return carry
        lax.fori_loop(0, depth, body, 0, unroll=depth)

    parts(0)
    for o in range(1, n_gx):
        gx_copy(o).wait_recv()
    total = slots_x[0]
    for i in range(1, n_gx):
        total = total + slots_x[i]
    mid[...] = total
    for o in range(1, n_gy):
        gy_copy(o).start()
    slots_y[gy] = total
    parts(1)
    for o in range(1, n_gy):
        gy_copy(o).wait_recv()
    total = slots_y[0]
    for i in range(1, n_gy):
        total = total + slots_y[i]
    total = jnp.where(diagonal, jnp.broadcast_to(total, (16, cols)), 0.0)
    total = jnp.broadcast_to(jnp.sum(total, axis=1, keepdims=True), (16, cols))

    coeffs = []
    for k in range(2):
        m = [total[8 * k + j:8 * k + j + 1, :] for j in range(6)]
        h = [SCALE * m[j + 1] + SHIFT * m[j] for j in range(5)]
        l1, l2 = h[1] / h[0], h[2] / h[0]
        a11, a12, a22 = h[2] - l1 * h[1], h[3] - l1 * h[2], h[4] - l2 * h[2]
        b1, b2 = m[1] - l1 * m[0], m[2] - l2 * m[0]
        l3 = a12 / a11
        c2 = (b2 - l3 * b1) / (a22 - l3 * a12)
        c1 = (b1 - a12 * c2) / a11
        c0 = (m[0] - h[1] * c1 - h[2] * c2) / h[0]
        coeffs.append([jnp.broadcast_to(c, (rows, cols)) for c in (c0, c1, c2)])

    for z in range(depth):
        grad = zero_tile
        for k in range(2):
            acc = zero_tile
            for j, v in enumerate((v0, v1, v2)):
                acc = acc + coeffs[k][j] * v[k, z + 1, 0:rows, 0:cols]
                grad = grad + coeffs[k][j] * gk[3 * k + j, z]
            adj_ref[k, z] = acc
        grad_ref[z] = -0.5 * grad

    for i, (dx, dy) in enumerate(sides):
        @pl.when(exists(dx, dy))
        def _():
            halo_copy(i).wait_send()
    for o in range(1, n_gx):
        gx_copy(o).wait_send()
    for o in range(1, n_gy):
        gy_copy(o).wait_send()


def solution(mesh):
    n_gx, n_gy = mesh.shape["gx"], mesh.shape["gy"]

    def per_device(conductance, labels, cotangent, saved):
        depth, rows, cols = conductance.shape
        f32 = jnp.float32
        big = (depth, 2 * rows, 2 * cols)
        padded = (2, depth + 2, 2 * rows, 2 * cols)
        face = depth * 13
        vmem = pl.BlockSpec(memory_space=pltpu.VMEM)
        dma = pltpu.SemaphoreType.DMA
        return pl.pallas_call(
            lambda *refs: kernel(n_gx, n_gy, *refs),
            out_shape=(
                jax.ShapeDtypeStruct(cotangent.shape, f32),
                jax.ShapeDtypeStruct(conductance.shape, f32),
            ),
            in_specs=[pl.BlockSpec(memory_space=pltpu.HBM)] * 4,
            out_specs=(vmem, vmem),
            scratch_shapes=[
                pltpu.VMEM(conductance.shape, f32),
                pltpu.VMEM(labels.shape, labels.dtype),
                pltpu.VMEM(cotangent.shape, f32),
                pltpu.VMEM(saved.shape, f32),
                dma((4,)),
                pltpu.VMEM(big, f32),
                pltpu.VMEM(big, f32),
                pltpu.VMEM((2,) + big, f32),
                pltpu.VMEM(padded, f32),
                pltpu.VMEM(padded, f32),
                pltpu.VMEM(padded, f32),
                pltpu.VMEM(big, f32),
                pltpu.VMEM(big, f32),
                pltpu.VMEM((depth + 1, 2 * rows, 2 * cols), f32),
                pltpu.VMEM(big, f32),
                pltpu.VMEM((6, depth, rows, cols), f32),
                pltpu.VMEM((2, face, cols), f32),
                pltpu.VMEM((2, face, cols), f32),
                pltpu.VMEM((6, rows, cols), f32),
                pltpu.VMEM((6, 6, rows, cols), f32),
                pltpu.VMEM((16, cols), f32),
                pltpu.VMEM((1, cols), f32),
                pltpu.VMEM((n_gx, 1, cols), f32),
                pltpu.VMEM((1, cols), f32),
                pltpu.VMEM((n_gy, 1, cols), f32),
                dma((8,)),
                dma((8,)),
                dma((n_gx,)),
                dma((n_gx,)),
                dma((n_gy,)),
                dma((n_gy,)),
            ],
            compiler_params=pltpu.CompilerParams(
                collective_id=0, has_side_effects=True, vmem_limit_bytes=32 * 1024 * 1024
            ),
        )(conductance, labels, cotangent, saved)

    return jax.shard_map(
        per_device,
        mesh=mesh,
        in_specs=(
            P(None, "gx", "gy"),
            P(None, "gx", "gy"),
            P(None, None, "gx", "gy"),
            P(None, None, "gx", "gy"),
        ),
        out_specs=(P(None, None, "gx", "gy"), P(None, "gx", "gy")),
        check_vma=False,
    )
```

```python
import jax
import jax.numpy as jnp
from jax import lax
from jax.experimental import pallas as pl
from jax.experimental.pallas import tpu as pltpu
from jax.sharding import PartitionSpec as P

SHIFT = 2.0
SCALE = 32.0
HALO = 3
MESH = pl.DeviceIdType.MESH


def kernel(
    n_gx, n_gy,
    cond_hbm, label_hbm, cot_hbm, saved_hbm,
    adj_ref, grad_ref,
    cond_ref, label_ref, cot_ref, saved_ref, in_sem,
    ce, me, pe, v0, v1, v2, wx, wy, wz, dd, gk,
    xsend, xrecv, ysend, yrecv, dsend, drecv, table, pay, slots,
    send_sem, recv_sem, sum_send, sum_recv,
):
    depth, rows, cols = cond_ref.shape
    R2, C2 = 2 * rows, 2 * cols
    gx = lax.axis_index("gx")
    gy = lax.axis_index("gy")
    has_up, has_down = gx > 0, gx < n_gx - 1
    has_left, has_right = gy > 0, gy < n_gy - 1

    sides = [(-1, 0), (1, 0), (0, -1), (0, 1), (-1, -1), (-1, 1), (1, -1), (1, 1)]

    def exists(dx, dy):
        ok = None
        for d, low, high in ((dx, has_up, has_down), (dy, has_left, has_right)):
            if d:
                here = low if d < 0 else high
                ok = here if ok is None else jnp.logical_and(ok, here)
        return ok

    count = n_gx * n_gy
    own = gx * n_gy + gy

    def peer(o):
        other = lax.rem(own + o, count)
        return lax.div(other, n_gy), lax.rem(other, n_gy)

    def each_peer(act):
        if count <= 64:
            for o in range(1, count):
                act(o)
        else:
            lax.fori_loop(1, count, lambda o, c: (act(o), c)[1], 0)

    fetches = [
        pltpu.make_async_copy(src, dst, in_sem.at[i])
        for i, (src, dst) in enumerate((
            (cond_hbm, cond_ref), (label_hbm, label_ref), (cot_hbm, cot_ref), (saved_hbm, saved_ref),
        ))
    ]
    for fetch in fetches:
        fetch.start()

    barrier = pltpu.get_barrier_semaphore()
    def greet(o):
        pl.semaphore_signal(barrier, inc=1, device_id=peer(o), device_id_type=MESH)

    each_peer(greet)

    zero_tile = jnp.zeros((rows, cols), jnp.float32)

    edge = jnp.zeros((R2, C2), jnp.float32)
    for v in (v0, v1, v2):
        for k in range(2):
            v[k, 0] = edge
            v[k, depth + 1] = edge
    wz[0] = edge
    for z in range(depth):
        for ref in (v0.at[0, z + 1], v0.at[1, z + 1], ce.at[z], me.at[z], pe.at[0, z], pe.at[1, z]):
            ref[rows:R2, 0:cols] = zero_tile
    for i, (dx, dy) in enumerate(sides):
        @pl.when(jnp.logical_not(exists(dx, dy)))
        def _():
            if i < 2:
                xrecv[i] = jnp.zeros(xrecv.shape[1:], jnp.float32)
            elif i < 4:
                yrecv[i - 2] = jnp.zeros(yrecv.shape[1:], jnp.float32)
            else:
                drecv[i - 4] = jnp.zeros(drecv.shape[1:], jnp.float32)

    for fetch in fetches:
        fetch.wait()

    def targets(z):
        return [v0.at[0, z + 1], v0.at[1, z + 1], ce.at[z], me.at[z], pe.at[0, z], pe.at[1, z]]

    for z in range(depth):
        lab = label_ref[z]
        m = jnp.where(lab == 0, 1.0, 0.0)
        fields = [m * cot_ref[0, z], m * cot_ref[1, z], cond_ref[z], m]
        for k in range(2):
            fields.append(jnp.where(lab == k + 1, 1.0, jnp.where(lab > 0, 0.0, saved_ref[k, z])))
        at = 0
        for f, ref, width in zip(fields, targets(z), (3, 3, 3, 2, 1, 1)):
            ref[0:rows, 0:cols] = f
            first = at + z * width
            xsend[0, first:first + width, :] = f[0:width]
            xsend[1, first:first + width, :] = f[rows - width:rows]
            at += depth * width

    pl.semaphore_wait(barrier, count - 1)

    def halo_copy(i):
        dx, dy = sides[i]
        back = sides.index((-dx, -dy))
        if dy == 0:
            src, dst = xsend.at[0 if dx < 0 else 1], xrecv.at[back]
        elif dx == 0:
            src, dst = ysend, yrecv.at[back - 2]
        else:
            src, dst = dsend.at[0 if dx < 0 else 1], drecv.at[back - 4]
        return pltpu.make_async_remote_copy(
            src_ref=src, dst_ref=dst, send_sem=send_sem.at[i], recv_sem=recv_sem.at[back],
            device_id=(gx + dx, gy + dy), device_id_type=MESH,
        )

    def arrival(i):
        dst = xrecv.at[i] if i < 2 else yrecv.at[i - 2] if i < 4 else drecv.at[i - 4]
        return pltpu.make_async_remote_copy(
            src_ref=dst, dst_ref=dst, send_sem=send_sem.at[i], recv_sem=recv_sem.at[i],
            device_id=(gx + sides[i][0], gy + sides[i][1]), device_id_type=MESH,
        )

    def send(first, end):
        for i in range(first, end):
            @pl.when(exists(*sides[i]))
            def _():
                halo_copy(i).start()

    def receive(first, end):
        for i in range(first, end):
            @pl.when(exists(*sides[i]))
            def _():
                arrival(i).wait_recv()

    send(0, 2)
    lane = lax.broadcasted_iota(jnp.int32, (rows, cols), 1)
    row = lax.broadcasted_iota(jnp.int32, (rows, cols), 0)
    slot_lanes = cols // depth
    packs = [zero_tile] * 6
    for z in range(depth):
        window = lax.rem(lane - z * slot_lanes + HALO + cols, cols) < 2 * HALO
        for i, ref in enumerate(targets(z)):
            f = ref[0:rows, 0:cols]
            rolled = pltpu.roll(f, z * slot_lanes, 1) if z else f
            packs[i] = jnp.where(window, rolled, packs[i])
    for i in range(6):
        ysend[i] = packs[i]
    send(2, 4)
    for j in range(2):
        one, other = packs[2 * j], packs[2 * j + 1]
        dsend[0, j] = jnp.where(row < HALO, one, pltpu.roll(other, HALO, 0))
        dsend[1, j] = jnp.where(row >= rows - HALO, one, pltpu.roll(other, rows - HALO, 0))
    send(4, 8)

    receive(2, 8)
    after = lax.rem(lane, slot_lanes) < HALO
    beside, corner = [], []
    for i in range(6):
        beside.append(jnp.where(after, yrecv[1, i], yrecv[0, i]))
        if i < 4:
            above = jnp.where(after, drecv[1, i // 2], drecv[0, i // 2])
            below = jnp.where(after, drecv[3, i // 2], drecv[2, i // 2])
            if i % 2:
                above = pltpu.roll(above, HALO, 0)
                below = pltpu.roll(below, rows - HALO, 0)
            corner.append(jnp.where(row < rows // 2, below, above))
    window = jnp.logical_or(lane < HALO, lane >= cols - HALO)
    corner_rows = jnp.logical_or(row < HALO, row >= rows - HALO)
    window_corner = jnp.logical_and(window, corner_rows)
    for z in range(depth):
        for f, ref in enumerate(targets(z)):
            back = (cols - z * slot_lanes) % cols
            tile = pltpu.roll(beside[f], back, 1) if back else beside[f]
            ref[0:rows, cols:C2] = jnp.where(window, tile, 0.0)
            if f < 4:
                tile = pltpu.roll(corner[f], back, 1) if back else corner[f]
                ref[rows:R2, cols:C2] = jnp.where(window_corner, tile, 0.0)

    receive(0, 2)

    for z in range(depth):
        at = 0
        for ref, width in zip(targets(z), (3, 3, 3, 2, 1, 1)):
            first = at + z * width
            ref[rows:rows + width, 0:cols] = xrecv[1, first:first + width, :]
            ref[R2 - width:R2, 0:cols] = xrecv[0, first:first + width, :]
            at += depth * width

    big_row = lax.broadcasted_iota(jnp.int32, (R2, C2), 0)
    big_lane = lax.broadcasted_iota(jnp.int32, (R2, C2), 1)
    no_x = jnp.logical_or(
        jnp.logical_and(big_row == rows - 1, jnp.logical_not(has_down)),
        jnp.logical_and(big_row == R2 - 1, jnp.logical_not(has_up)),
    )
    no_y = jnp.logical_or(
        jnp.logical_and(big_lane == cols - 1, jnp.logical_not(has_right)),
        jnp.logical_and(big_lane == C2 - 1, jnp.logical_not(has_left)),
    )
    valid_x = jnp.where(no_x, 0.0, 1.0)
    valid_y = jnp.where(no_y, 0.0, 1.0)
    half_x = valid_x * (0.5 / SCALE)
    half_y = valid_y * (0.5 / SCALE)
    last = depth - 1

    def next_row(a):
        return pltpu.roll(a, a.shape[0] - 1, 0)

    def next_lane(a):
        return pltpu.roll(a, a.shape[1] - 1, 1)

    def weights(z, carry):
        c = ce[z]
        ex = half_x * (c + next_row(c))
        ey = half_y * (c + next_lane(c))
        cn = ce[jnp.minimum(z + 1, last)]
        ez = jnp.where(z < last, 0.5 / SCALE, 0.0) * (c + cn)
        wx[z] = ex
        wy[z] = ey
        wz[z + 1] = ez
        deg = ex + pltpu.roll(ex, 1, 0) + ey + pltpu.roll(ey, 1, 1) + ez + wz[z]
        dd[z] = deg + (1.0 - SHIFT) / SCALE
        return carry

    lax.fori_loop(0, depth, weights, 0, unroll=depth)

    def apply_full(src, dst, sums):
        def body(z, carry):
            ex, ey, ez, ezm, d, m = wx[z], wy[z], wz[z + 1], wz[z], dd[z], me[z]
            out = []
            for k in range(2):
                v = src[k, z + 1]
                a = d * v - ez * src[k, z + 2] - ezm * src[k, z]
                a = a - ex * next_row(v) - pltpu.roll(ex * v, 1, 0)
                a = a - ey * next_lane(v) - pltpu.roll(ey * v, 1, 1)
                a = m * a
                dst[k, z + 1] = a
                old, new = v[0:rows, 0:cols], a[0:rows, 0:cols]
                out.append(carry[3 * k] + old * old)
                out.append(carry[3 * k + 1] + old * new)
                out.append(carry[3 * k + 2] + new * new)
            return tuple(out)
        return lax.fori_loop(0, depth, body, (zero_tile,) * 6, unroll=depth)

    first = apply_full(v0, v1, True)
    second = apply_full(v1, v2, True)

    def apply_core(z, carry):
        exr = wx[z, :, 0:cols]
        eyr = wy[z, 0:rows, :]
        ez, ezm = wz[z + 1, 0:rows, 0:cols], wz[z, 0:rows, 0:cols]
        d, m = dd[z, 0:rows, 0:cols], me[z, 0:rows, 0:cols]
        out = []
        for k in range(2):
            vx = v2[k, z + 1, :, 0:cols]
            vy = v2[k, z + 1, 0:rows, :]
            v = vx[0:rows]
            a = d * v - ez * v2[k, z + 2, 0:rows, 0:cols] - ezm * v2[k, z, 0:rows, 0:cols]
            a = a - (exr * next_row(vx) + pltpu.roll(exr * vx, 1, 0))[0:rows]
            a = a - (eyr * next_lane(vy) + pltpu.roll(eyr * vy, 1, 1))[:, 0:cols]
            out.append(carry[k] + v * (m * a))
        return tuple(out)

    third = lax.fori_loop(0, depth, apply_core, (zero_tile,) * 2, unroll=depth)

    for k in range(2):
        moments = [first[3 * k], first[3 * k + 1], first[3 * k + 2],
                   second[3 * k + 1], second[3 * k + 2], third[k]]
        for j, a in enumerate(moments):
            table[8 * k + j:8 * k + j + 1, :] = jnp.sum(a, axis=0, keepdims=True)
        table[8 * k + 6:8 * k + 8, :] = jnp.zeros((2, cols), jnp.float32)
    diagonal = lax.broadcasted_iota(jnp.int32, (16, cols), 0) == lax.broadcasted_iota(jnp.int32, (16, cols), 1)
    sums = jnp.broadcast_to(jnp.sum(table[...], axis=1, keepdims=True), (16, cols))
    pay[...] = jnp.sum(jnp.where(diagonal, sums, 0.0), axis=0, keepdims=True)

    def sum_copy(o):
        return pltpu.make_async_remote_copy(
            src_ref=pay, dst_ref=slots.at[own], send_sem=sum_send.at[o], recv_sem=sum_recv.at[o],
            device_id=peer(o), device_id_type=MESH,
        )

    each_peer(lambda o: sum_copy(o).start())
    slots[own] = pay[...]

    vx_edge = valid_x[:, 0:cols]
    vy_edge = valid_y[0:rows, :]

    def parts(k):
        def body(z, carry):
            up = jnp.minimum(z + 1, last)
            down = jnp.maximum(z - 1, 0)
            px = pe[k, z, :, 0:cols]
            py = pe[k, z, 0:rows, :]
            p = px[0:rows]
            dx = vx_edge * (px - next_row(px))
            dy = vy_edge * (py - next_lane(py))
            du = p - pe[k, up, 0:rows, 0:cols]
            dn = p - pe[k, down, 0:rows, 0:cols]
            for j, v in enumerate((v0, v1, v2)):
                ax = v[k, z + 1, :, 0:cols]
                ay = v[k, z + 1, 0:rows, :]
                a = ax[0:rows]
                qx = dx * (ax - next_row(ax))
                qy = dy * (ay - next_lane(ay))
                g = qx[0:rows] + pltpu.roll(qx, 1, 0)[0:rows]
                g = g + qy[:, 0:cols] + pltpu.roll(qy, 1, 1)[:, 0:cols]
                g = g + du * (a - v[k, z + 2, 0:rows, 0:cols])
                g = g + dn * (a - v[k, z, 0:rows, 0:cols])
                gk[3 * k + j, z] = g
            return carry
        lax.fori_loop(0, depth, body, 0, unroll=depth)

    parts(0)
    parts(1)
    each_peer(lambda o: sum_copy(o).wait_recv())
    total = jnp.sum(slots[...], axis=0)
    total = jnp.where(diagonal, jnp.broadcast_to(total, (16, cols)), 0.0)
    total = jnp.broadcast_to(jnp.sum(total, axis=1, keepdims=True), (16, cols))

    coeffs = []
    for k in range(2):
        m = [total[8 * k + j:8 * k + j + 1, :] for j in range(6)]
        h = [SCALE * m[j + 1] + SHIFT * m[j] for j in range(5)]
        l1, l2 = h[1] / h[0], h[2] / h[0]
        a11, a12, a22 = h[2] - l1 * h[1], h[3] - l1 * h[2], h[4] - l2 * h[2]
        b1, b2 = m[1] - l1 * m[0], m[2] - l2 * m[0]
        l3 = a12 / a11
        c2 = (b2 - l3 * b1) / (a22 - l3 * a12)
        c1 = (b1 - a12 * c2) / a11
        c0 = (m[0] - h[1] * c1 - h[2] * c2) / h[0]
        coeffs.append([jnp.broadcast_to(c, (rows, cols)) for c in (c0, c1, c2)])

    for z in range(depth):
        grad = zero_tile
        for k in range(2):
            acc = zero_tile
            for j, v in enumerate((v0, v1, v2)):
                acc = acc + coeffs[k][j] * v[k, z + 1, 0:rows, 0:cols]
                grad = grad + coeffs[k][j] * gk[3 * k + j, z]
            adj_ref[k, z] = acc
        grad_ref[z] = -0.5 * grad

    for i, (dx, dy) in enumerate(sides):
        @pl.when(exists(dx, dy))
        def _():
            halo_copy(i).wait_send()
    each_peer(lambda o: sum_copy(o).wait_send())


def solution(mesh):
    n_gx, n_gy = mesh.shape["gx"], mesh.shape["gy"]

    def per_device(conductance, labels, cotangent, saved):
        depth, rows, cols = conductance.shape
        f32 = jnp.float32
        big = (depth, 2 * rows, 2 * cols)
        padded = (2, depth + 2, 2 * rows, 2 * cols)
        face = depth * 13
        vmem = pl.BlockSpec(memory_space=pltpu.VMEM)
        dma = pltpu.SemaphoreType.DMA
        return pl.pallas_call(
            lambda *refs: kernel(n_gx, n_gy, *refs),
            out_shape=(
                jax.ShapeDtypeStruct(cotangent.shape, f32),
                jax.ShapeDtypeStruct(conductance.shape, f32),
            ),
            in_specs=[pl.BlockSpec(memory_space=pltpu.HBM)] * 4,
            out_specs=(vmem, vmem),
            scratch_shapes=[
                pltpu.VMEM(conductance.shape, f32),
                pltpu.VMEM(labels.shape, labels.dtype),
                pltpu.VMEM(cotangent.shape, f32),
                pltpu.VMEM(saved.shape, f32),
                dma((4,)),
                pltpu.VMEM(big, f32),
                pltpu.VMEM(big, f32),
                pltpu.VMEM((2,) + big, f32),
                pltpu.VMEM(padded, f32),
                pltpu.VMEM(padded, f32),
                pltpu.VMEM(padded, f32),
                pltpu.VMEM(big, f32),
                pltpu.VMEM(big, f32),
                pltpu.VMEM((depth + 1, 2 * rows, 2 * cols), f32),
                pltpu.VMEM(big, f32),
                pltpu.VMEM((6, depth, rows, cols), f32),
                pltpu.VMEM((2, face, cols), f32),
                pltpu.VMEM((2, face, cols), f32),
                pltpu.VMEM((6, rows, cols), f32),
                pltpu.VMEM((2, 6, rows, cols), f32),
                pltpu.VMEM((2, 2, rows, cols), f32),
                pltpu.VMEM((4, 2, rows, cols), f32),
                pltpu.VMEM((16, cols), f32),
                pltpu.VMEM((1, cols), f32),
                pltpu.VMEM((n_gx * n_gy, 1, cols), f32),
                dma((8,)),
                dma((8,)),
                dma((n_gx * n_gy,)),
                dma((n_gx * n_gy,)),
            ],
            compiler_params=pltpu.CompilerParams(
                collective_id=0, has_side_effects=True, vmem_limit_bytes=32 * 1024 * 1024
            ),
        )(conductance, labels, cotangent, saved)

    return jax.shard_map(
        per_device,
        mesh=mesh,
        in_specs=(
            P(None, "gx", "gy"),
            P(None, "gx", "gy"),
            P(None, None, "gx", "gy"),
            P(None, None, "gx", "gy"),
        ),
        out_specs=(P(None, None, "gx", "gy"), P(None, "gx", "gy")),
        check_vma=False,
    )
```

```python
import jax
import jax.numpy as jnp
from jax import lax
from jax.experimental import pallas as pl
from jax.experimental.pallas import tpu as pltpu
from jax.sharding import PartitionSpec as P

SHIFT = 2.0
SCALE = 32.0
HALO = 3
MESH = pl.DeviceIdType.MESH


def kernel(
    n_gx, n_gy,
    cond_hbm, label_hbm, cot_hbm, saved_hbm,
    adj_ref, grad_ref,
    cond_ref, label_ref, cot_ref, saved_ref, in_sem,
    ce, me, pe, v0, v1, v2, wx, wy, wz, dd, gk,
    xsend, xrecv, ysend, yrecv, dsend, drecv, table, pay, slots_x, mid, slots_y,
    send_sem, recv_sem, gx_send, gx_recv, gy_send, gy_recv,
):
    depth, rows, cols = cond_ref.shape
    R2, C2 = 2 * rows, 2 * cols
    gx = lax.axis_index("gx")
    gy = lax.axis_index("gy")
    has_up, has_down = gx > 0, gx < n_gx - 1
    has_left, has_right = gy > 0, gy < n_gy - 1

    sides = [(-1, 0), (1, 0), (0, -1), (0, 1), (-1, -1), (-1, 1), (1, -1), (1, 1)]

    def exists(dx, dy):
        ok = None
        for d, low, high in ((dx, has_up, has_down), (dy, has_left, has_right)):
            if d:
                here = low if d < 0 else high
                ok = here if ok is None else jnp.logical_and(ok, here)
        return ok

    fetches = [
        pltpu.make_async_copy(src, dst, in_sem.at[i])
        for i, (src, dst) in enumerate((
            (cond_hbm, cond_ref), (label_hbm, label_ref), (cot_hbm, cot_ref), (saved_hbm, saved_ref),
        ))
    ]
    for fetch in fetches:
        fetch.start()

    barrier = pltpu.get_barrier_semaphore()
    partners = n_gx - 1 + n_gy - 1
    for dx, dy in sides[4:]:
        partners = partners + jnp.where(exists(dx, dy), 1, 0)

        @pl.when(exists(dx, dy))
        def _():
            pl.semaphore_signal(barrier, inc=1, device_id=(gx + dx, gy + dy), device_id_type=MESH)
    for o in range(1, n_gy):
        pl.semaphore_signal(barrier, inc=1, device_id=(gx, lax.rem(gy + o, n_gy)), device_id_type=MESH)
    for o in range(1, n_gx):
        pl.semaphore_signal(barrier, inc=1, device_id=(lax.rem(gx + o, n_gx), gy), device_id_type=MESH)

    zero_tile = jnp.zeros((rows, cols), jnp.float32)

    edge = jnp.zeros((R2, C2), jnp.float32)
    for v in (v0, v1, v2):
        for k in range(2):
            v[k, 0] = edge
            v[k, depth + 1] = edge
    wz[0] = edge
    for z in range(depth):
        for ref in (v0.at[0, z + 1], v0.at[1, z + 1], ce.at[z], me.at[z], pe.at[0, z], pe.at[1, z]):
            ref[rows:R2, 0:cols] = zero_tile
    for i, (dx, dy) in enumerate(sides):
        @pl.when(jnp.logical_not(exists(dx, dy)))
        def _():
            if i < 2:
                xrecv[i] = jnp.zeros(xrecv.shape[1:], jnp.float32)
            elif i < 4:
                yrecv[i - 2] = jnp.zeros(yrecv.shape[1:], jnp.float32)
            else:
                drecv[i - 4] = jnp.zeros(drecv.shape[1:], jnp.float32)

    for fetch in fetches:
        fetch.wait()

    half = depth // 2

    def targets(z):
        return [v0.at[0, z + 1], v0.at[1, z + 1], ce.at[z], me.at[z], pe.at[0, z], pe.at[1, z]]

    for z in range(depth):
        lab = label_ref[z]
        m = jnp.where(lab == 0, 1.0, 0.0)
        fields = [m * cot_ref[0, z], m * cot_ref[1, z], cond_ref[z], m]
        for k in range(2):
            fields.append(jnp.where(lab == k + 1, 1.0, jnp.where(lab > 0, 0.0, saved_ref[k, z])))
        piece, at = z // half, 0
        for f, ref, width in zip(fields, targets(z), (3, 3, 3, 2, 1, 1)):
            ref[0:rows, 0:cols] = f
            first = at + z % half * width
            xsend[0, piece, first:first + width, :] = f[0:width]
            xsend[1, piece, first:first + width, :] = f[rows - width:rows]
            at += half * width

    pl.semaphore_wait(barrier, partners)

    def remote(i, src, dst, send_at, recv_at):
        return pltpu.make_async_remote_copy(
            src_ref=src, dst_ref=dst, send_sem=send_sem.at[send_at], recv_sem=recv_sem.at[recv_at],
            device_id=(gx + sides[i][0], gy + sides[i][1]), device_id_type=MESH,
        )

    def halo_copies(i):
        dx, dy = sides[i]
        back = sides.index((-dx, -dy))
        if dy == 0:
            return [
                remote(i, xsend.at[i, p], xrecv.at[back, p], i + 8 * p, back + 8 * p) for p in range(2)
            ]
        if dx == 0:
            return [remote(i, ysend, yrecv.at[back - 2], i, back)]
        return [remote(i, dsend.at[0 if dx < 0 else 1], drecv.at[back - 4], i, back)]

    def send(first, end, p=0):
        for i in range(first, end):
            @pl.when(exists(*sides[i]))
            def _():
                halo_copies(i)[p].start()

    def receive(first, end, p=0):
        for i in range(first, end):
            @pl.when(exists(*sides[i]))
            def _():
                dst = xrecv.at[i, p] if i < 2 else yrecv.at[i - 2] if i < 4 else drecv.at[i - 4]
                remote(i, dst, dst, i + 8 * p, i + 8 * p).wait_recv()

    send(0, 2)
    send(0, 2, 1)
    lane = lax.broadcasted_iota(jnp.int32, (rows, cols), 1)
    row = lax.broadcasted_iota(jnp.int32, (rows, cols), 0)
    slot_lanes = cols // depth
    packs = [zero_tile] * 6
    for z in range(depth):
        window = lax.rem(lane - z * slot_lanes + HALO + cols, cols) < 2 * HALO
        for i, ref in enumerate(targets(z)):
            f = ref[0:rows, 0:cols]
            rolled = pltpu.roll(f, z * slot_lanes, 1) if z else f
            packs[i] = jnp.where(window, rolled, packs[i])
    for i in range(6):
        ysend[i] = packs[i]
    send(2, 4)
    for j in range(2):
        one, other = packs[2 * j], packs[2 * j + 1]
        dsend[0, j] = jnp.where(row < HALO, one, pltpu.roll(other, HALO, 0))
        dsend[1, j] = jnp.where(row >= rows - HALO, one, pltpu.roll(other, rows - HALO, 0))
    send(4, 8)

    receive(2, 4)
    after = lax.rem(lane, slot_lanes) < HALO
    window = jnp.logical_or(lane < HALO, lane >= cols - HALO)
    corner_rows = jnp.logical_or(row < HALO, row >= rows - HALO)
    window_corner = jnp.logical_and(window, corner_rows)

    def unroll_lanes(tile, z):
        back = (cols - z * slot_lanes) % cols
        return pltpu.roll(tile, back, 1) if back else tile

    beside = [jnp.where(after, yrecv[1, i], yrecv[0, i]) for i in range(6)]
    for z in range(depth):
        for f, ref in enumerate(targets(z)):
            ref[0:rows, cols:C2] = jnp.where(window, unroll_lanes(beside[f], z), 0.0)

    receive(4, 8)
    corner = []
    for i in range(4):
        above = jnp.where(after, drecv[1, i // 2], drecv[0, i // 2])
        below = jnp.where(after, drecv[3, i // 2], drecv[2, i // 2])
        if i % 2:
            above = pltpu.roll(above, HALO, 0)
            below = pltpu.roll(below, rows - HALO, 0)
        corner.append(jnp.where(row < rows // 2, below, above))
    for z in range(depth):
        for f, ref in enumerate(targets(z)[:4]):
            ref[rows:R2, cols:C2] = jnp.where(window_corner, unroll_lanes(corner[f], z), 0.0)

    def unpack_x(p):
        for z in range(half):
            at = 0
            for ref, width in zip(targets(p * half + z), (3, 3, 3, 2, 1, 1)):
                first = at + z * width
                ref[rows:rows + width, 0:cols] = xrecv[1, p, first:first + width, :]
                ref[R2 - width:R2, 0:cols] = xrecv[0, p, first:first + width, :]
                at += half * width

    big_row = lax.broadcasted_iota(jnp.int32, (R2, C2), 0)
    big_lane = lax.broadcasted_iota(jnp.int32, (R2, C2), 1)
    no_x = jnp.logical_or(
        jnp.logical_and(big_row == rows - 1, jnp.logical_not(has_down)),
        jnp.logical_and(big_row == R2 - 1, jnp.logical_not(has_up)),
    )
    no_y = jnp.logical_or(
        jnp.logical_and(big_lane == cols - 1, jnp.logical_not(has_right)),
        jnp.logical_and(big_lane == C2 - 1, jnp.logical_not(has_left)),
    )
    valid_x = jnp.where(no_x, 0.0, 1.0)
    valid_y = jnp.where(no_y, 0.0, 1.0)
    half_x = valid_x * (0.5 / SCALE)
    half_y = valid_y * (0.5 / SCALE)
    last = depth - 1

    def next_row(a):
        return pltpu.roll(a, a.shape[0] - 1, 0)

    def next_lane(a):
        return pltpu.roll(a, a.shape[1] - 1, 1)

    def weights(z, carry):
        c = ce[z]
        ex = half_x * (c + next_row(c))
        ey = half_y * (c + next_lane(c))
        cn = ce[jnp.minimum(z + 1, last)]
        ez = jnp.where(z < last, 0.5 / SCALE, 0.0) * (c + cn)
        wx[z] = ex
        wy[z] = ey
        wz[z + 1] = ez
        deg = ex + pltpu.roll(ex, 1, 0) + ey + pltpu.roll(ey, 1, 1) + ez + wz[z]
        dd[z] = deg + (1.0 - SHIFT) / SCALE
        return carry

    def apply_full(src, dst, start, end, sums):
        def body(z, carry):
            ex, ey, ez, ezm, d, m = wx[z], wy[z], wz[z + 1], wz[z], dd[z], me[z]
            out = []
            for k in range(2):
                v = src[k, z + 1]
                a = d * v - ez * src[k, z + 2] - ezm * src[k, z]
                a = a - ex * next_row(v) - pltpu.roll(ex * v, 1, 0)
                a = a - ey * next_lane(v) - pltpu.roll(ey * v, 1, 1)
                a = m * a
                dst[k, z + 1] = a
                old, new = v[0:rows, 0:cols], a[0:rows, 0:cols]
                out.append(carry[3 * k] + old * old)
                out.append(carry[3 * k + 1] + old * new)
                out.append(carry[3 * k + 2] + new * new)
            return tuple(out)
        return lax.fori_loop(start, end, body, sums, unroll=end - start)

    zero_sums = (zero_tile,) * 6
    receive(0, 2)
    unpack_x(0)
    lax.fori_loop(0, half - 1, weights, 0, unroll=half - 1)
    first = apply_full(v0, v1, 0, half - 1, zero_sums)
    receive(0, 2, 1)
    unpack_x(1)
    lax.fori_loop(half - 1, depth, weights, 0, unroll=depth - half + 1)
    first = apply_full(v0, v1, half - 1, depth, first)
    second = apply_full(v1, v2, 0, depth, zero_sums)

    def apply_core(z, carry):
        exr = wx[z, :, 0:cols]
        eyr = wy[z, 0:rows, :]
        ez, ezm = wz[z + 1, 0:rows, 0:cols], wz[z, 0:rows, 0:cols]
        d, m = dd[z, 0:rows, 0:cols], me[z, 0:rows, 0:cols]
        out = []
        for k in range(2):
            vx = v2[k, z + 1, :, 0:cols]
            vy = v2[k, z + 1, 0:rows, :]
            v = vx[0:rows]
            a = d * v - ez * v2[k, z + 2, 0:rows, 0:cols] - ezm * v2[k, z, 0:rows, 0:cols]
            a = a - (exr * next_row(vx) + pltpu.roll(exr * vx, 1, 0))[0:rows]
            a = a - (eyr * next_lane(vy) + pltpu.roll(eyr * vy, 1, 1))[:, 0:cols]
            out.append(carry[k] + v * (m * a))
        return tuple(out)

    third = lax.fori_loop(0, depth, apply_core, (zero_tile,) * 2, unroll=depth)

    for k in range(2):
        moments = [first[3 * k], first[3 * k + 1], first[3 * k + 2],
                   second[3 * k + 1], second[3 * k + 2], third[k]]
        for j, a in enumerate(moments):
            table[8 * k + j:8 * k + j + 1, :] = jnp.sum(a, axis=0, keepdims=True)
        table[8 * k + 6:8 * k + 8, :] = jnp.zeros((2, cols), jnp.float32)
    diagonal = lax.broadcasted_iota(jnp.int32, (16, cols), 0) == lax.broadcasted_iota(jnp.int32, (16, cols), 1)
    sums = jnp.broadcast_to(jnp.sum(table[...], axis=1, keepdims=True), (16, cols))
    pay[...] = jnp.sum(jnp.where(diagonal, sums, 0.0), axis=0, keepdims=True)

    def gx_copy(o):
        return pltpu.make_async_remote_copy(
            src_ref=pay, dst_ref=slots_x.at[gx], send_sem=gx_send.at[o], recv_sem=gx_recv.at[o],
            device_id=(lax.rem(gx + o, n_gx), gy), device_id_type=MESH,
        )

    def gy_copy(o):
        return pltpu.make_async_remote_copy(
            src_ref=mid, dst_ref=slots_y.at[gy], send_sem=gy_send.at[o], recv_sem=gy_recv.at[o],
            device_id=(gx, lax.rem(gy + o, n_gy)), device_id_type=MESH,
        )

    for o in range(1, n_gx):
        gx_copy(o).start()
    slots_x[gx] = pay[...]

    vx_edge = valid_x[:, 0:cols]
    vy_edge = valid_y[0:rows, :]

    def parts(k):
        def body(z, carry):
            up = jnp.minimum(z + 1, last)
            down = jnp.maximum(z - 1, 0)
            px = pe[k, z, :, 0:cols]
            py = pe[k, z, 0:rows, :]
            p = px[0:rows]
            dx = vx_edge * (px - next_row(px))
            dy = vy_edge * (py - next_lane(py))
            du = p - pe[k, up, 0:rows, 0:cols]
            dn = p - pe[k, down, 0:rows, 0:cols]
            for j, v in enumerate((v0, v1, v2)):
                ax = v[k, z + 1, :, 0:cols]
                ay = v[k, z + 1, 0:rows, :]
                a = ax[0:rows]
                qx = dx * (ax - next_row(ax))
                qy = dy * (ay - next_lane(ay))
                g = qx[0:rows] + pltpu.roll(qx, 1, 0)[0:rows]
                g = g + qy[:, 0:cols] + pltpu.roll(qy, 1, 1)[:, 0:cols]
                g = g + du * (a - v[k, z + 2, 0:rows, 0:cols])
                g = g + dn * (a - v[k, z, 0:rows, 0:cols])
                gk[3 * k + j, z] = g
            return carry
        lax.fori_loop(0, depth, body, 0, unroll=depth)

    parts(0)
    for o in range(1, n_gx):
        gx_copy(o).wait_recv()
    total = jnp.sum(slots_x[...], axis=0)
    mid[...] = total
    for o in range(1, n_gy):
        gy_copy(o).start()
    slots_y[gy] = total
    parts(1)
    for o in range(1, n_gy):
        gy_copy(o).wait_recv()
    total = jnp.sum(slots_y[...], axis=0)
    total = jnp.where(diagonal, jnp.broadcast_to(total, (16, cols)), 0.0)
    total = jnp.broadcast_to(jnp.sum(total, axis=1, keepdims=True), (16, cols))

    coeffs = []
    for k in range(2):
        m = [total[8 * k + j:8 * k + j + 1, :] for j in range(6)]
        h = [SCALE * m[j + 1] + SHIFT * m[j] for j in range(5)]
        l1, l2 = h[1] / h[0], h[2] / h[0]
        a11, a12, a22 = h[2] - l1 * h[1], h[3] - l1 * h[2], h[4] - l2 * h[2]
        b1, b2 = m[1] - l1 * m[0], m[2] - l2 * m[0]
        l3 = a12 / a11
        c2 = (b2 - l3 * b1) / (a22 - l3 * a12)
        c1 = (b1 - a12 * c2) / a11
        c0 = (m[0] - h[1] * c1 - h[2] * c2) / h[0]
        coeffs.append([jnp.broadcast_to(c, (rows, cols)) for c in (c0, c1, c2)])

    for z in range(depth):
        grad = zero_tile
        for k in range(2):
            acc = zero_tile
            for j, v in enumerate((v0, v1, v2)):
                acc = acc + coeffs[k][j] * v[k, z + 1, 0:rows, 0:cols]
                grad = grad + coeffs[k][j] * gk[3 * k + j, z]
            adj_ref[k, z] = acc
        grad_ref[z] = -0.5 * grad

    for i, (dx, dy) in enumerate(sides):
        @pl.when(exists(dx, dy))
        def _():
            for copy in halo_copies(i):
                copy.wait_send()
    for o in range(1, n_gx):
        gx_copy(o).wait_send()
    for o in range(1, n_gy):
        gy_copy(o).wait_send()


def solution(mesh):
    n_gx, n_gy = mesh.shape["gx"], mesh.shape["gy"]

    def per_device(conductance, labels, cotangent, saved):
        depth, rows, cols = conductance.shape
        f32 = jnp.float32
        big = (depth, 2 * rows, 2 * cols)
        padded = (2, depth + 2, 2 * rows, 2 * cols)
        face = (2, 2, depth // 2 * 13, cols)
        vmem = pl.BlockSpec(memory_space=pltpu.VMEM)
        dma = pltpu.SemaphoreType.DMA
        return pl.pallas_call(
            lambda *refs: kernel(n_gx, n_gy, *refs),
            out_shape=(
                jax.ShapeDtypeStruct(cotangent.shape, f32),
                jax.ShapeDtypeStruct(conductance.shape, f32),
            ),
            in_specs=[pl.BlockSpec(memory_space=pltpu.HBM)] * 4,
            out_specs=(vmem, vmem),
            scratch_shapes=[
                pltpu.VMEM(conductance.shape, f32),
                pltpu.VMEM(labels.shape, labels.dtype),
                pltpu.VMEM(cotangent.shape, f32),
                pltpu.VMEM(saved.shape, f32),
                dma((4,)),
                pltpu.VMEM(big, f32),
                pltpu.VMEM(big, f32),
                pltpu.VMEM((2,) + big, f32),
                pltpu.VMEM(padded, f32),
                pltpu.VMEM(padded, f32),
                pltpu.VMEM(padded, f32),
                pltpu.VMEM(big, f32),
                pltpu.VMEM(big, f32),
                pltpu.VMEM((depth + 1, 2 * rows, 2 * cols), f32),
                pltpu.VMEM(big, f32),
                pltpu.VMEM((6, depth, rows, cols), f32),
                pltpu.VMEM(face, f32),
                pltpu.VMEM(face, f32),
                pltpu.VMEM((6, rows, cols), f32),
                pltpu.VMEM((2, 6, rows, cols), f32),
                pltpu.VMEM((2, 2, rows, cols), f32),
                pltpu.VMEM((4, 2, rows, cols), f32),
                pltpu.VMEM((16, cols), f32),
                pltpu.VMEM((1, cols), f32),
                pltpu.VMEM((n_gx, 1, cols), f32),
                pltpu.VMEM((1, cols), f32),
                pltpu.VMEM((n_gy, 1, cols), f32),
                dma((10,)),
                dma((10,)),
                dma((n_gx,)),
                dma((n_gx,)),
                dma((n_gy,)),
                dma((n_gy,)),
            ],
            compiler_params=pltpu.CompilerParams(
                collective_id=0, has_side_effects=True, vmem_limit_bytes=32 * 1024 * 1024
            ),
        )(conductance, labels, cotangent, saved)

    return jax.shard_map(
        per_device,
        mesh=mesh,
        in_specs=(
            P(None, "gx", "gy"),
            P(None, "gx", "gy"),
            P(None, None, "gx", "gy"),
            P(None, None, "gx", "gy"),
        ),
        out_specs=(P(None, None, "gx", "gy"), P(None, "gx", "gy")),
        check_vma=False,
    )
```

```python
import jax
import jax.numpy as jnp
from jax import lax
from jax.experimental import pallas as pl
from jax.experimental.pallas import tpu as pltpu
from jax.sharding import PartitionSpec as P

SHIFT = 2.0
SCALE = 32.0
HALO = 3
MESH = pl.DeviceIdType.MESH


def kernel(
    n_gx, n_gy,
    cond_hbm, label_hbm, cot_hbm, saved_hbm,
    adj_ref, grad_ref,
    cond_ref, label_ref, cot_ref, saved_ref, in_sem,
    ce, me, pe, v0, v1, v2, wx, wy, wz, dd, gk,
    xsend, xrecv, ysend, yrecv, dsend, drecv, table, pay, slots_x, mid, slots_y,
    send_sem, recv_sem, gx_send, gx_recv, gy_send, gy_recv,
):
    depth, rows, cols = cond_ref.shape
    R2, C2 = 2 * rows, 2 * cols
    gx = lax.axis_index("gx")
    gy = lax.axis_index("gy")
    has_up, has_down = gx > 0, gx < n_gx - 1
    has_left, has_right = gy > 0, gy < n_gy - 1

    sides = [(-1, 0), (1, 0), (0, -1), (0, 1), (-1, -1), (-1, 1), (1, -1), (1, 1)]

    def exists(dx, dy):
        ok = None
        for d, low, high in ((dx, has_up, has_down), (dy, has_left, has_right)):
            if d:
                here = low if d < 0 else high
                ok = here if ok is None else jnp.logical_and(ok, here)
        return ok

    fetches = [
        pltpu.make_async_copy(src, dst, in_sem.at[i])
        for i, (src, dst) in enumerate((
            (cond_hbm, cond_ref), (label_hbm, label_ref), (cot_hbm, cot_ref), (saved_hbm, saved_ref),
        ))
    ]
    for fetch in fetches:
        fetch.start()

    barrier = pltpu.get_barrier_semaphore()
    partners = n_gx - 1 + n_gy - 1
    for dx, dy in sides[4:]:
        partners = partners + jnp.where(exists(dx, dy), 1, 0)

        @pl.when(exists(dx, dy))
        def _():
            pl.semaphore_signal(barrier, inc=1, device_id=(gx + dx, gy + dy), device_id_type=MESH)
    for o in range(1, n_gy):
        pl.semaphore_signal(barrier, inc=1, device_id=(gx, lax.rem(gy + o, n_gy)), device_id_type=MESH)
    for o in range(1, n_gx):
        pl.semaphore_signal(barrier, inc=1, device_id=(lax.rem(gx + o, n_gx), gy), device_id_type=MESH)

    zero_tile = jnp.zeros((rows, cols), jnp.float32)

    edge = jnp.zeros((R2, C2), jnp.float32)
    for v in (v0, v1, v2):
        for k in range(2):
            v[k, 0] = edge
            v[k, depth + 1] = edge
    wz[0] = edge
    for z in range(depth):
        for ref in (v0.at[0, z + 1], v0.at[1, z + 1], ce.at[z], me.at[z], pe.at[0, z], pe.at[1, z]):
            ref[rows:R2, 0:cols] = zero_tile
    for i, (dx, dy) in enumerate(sides):
        @pl.when(jnp.logical_not(exists(dx, dy)))
        def _():
            if i < 2:
                xrecv[i] = jnp.zeros(xrecv.shape[1:], jnp.float32)
            elif i < 4:
                yrecv[i - 2] = jnp.zeros(yrecv.shape[1:], jnp.float32)
            else:
                drecv[i - 4] = jnp.zeros(drecv.shape[1:], jnp.float32)

    for fetch in fetches:
        fetch.wait()

    half = depth // 2

    def targets(z):
        return [v0.at[0, z + 1], v0.at[1, z + 1], ce.at[z], me.at[z], pe.at[0, z], pe.at[1, z]]

    for z in range(depth):
        lab = label_ref[z]
        m = jnp.where(lab == 0, 1.0, 0.0)
        fields = [m * cot_ref[0, z], m * cot_ref[1, z], cond_ref[z], m]
        for k in range(2):
            fields.append(jnp.where(lab == k + 1, 1.0, jnp.where(lab > 0, 0.0, saved_ref[k, z])))
        piece, at = z // half, 0
        for f, ref, width in zip(fields, targets(z), (3, 3, 3, 2, 1, 1)):
            ref[0:rows, 0:cols] = f
            first = at + z % half * width
            xsend[0, piece, first:first + width, :] = f[0:width]
            xsend[1, piece, first:first + width, :] = f[rows - width:rows]
            at += half * width

    pl.semaphore_wait(barrier, partners)

    def remote(i, src, dst, send_at, recv_at):
        return pltpu.make_async_remote_copy(
            src_ref=src, dst_ref=dst, send_sem=send_sem.at[send_at], recv_sem=recv_sem.at[recv_at],
            device_id=(gx + sides[i][0], gy + sides[i][1]), device_id_type=MESH,
        )

    def halo_copies(i):
        dx, dy = sides[i]
        back = sides.index((-dx, -dy))
        if dy == 0:
            return [
                remote(i, xsend.at[i, p], xrecv.at[back, p], i + 8 * p, back + 8 * p) for p in range(2)
            ]
        if dx == 0:
            return [remote(i, ysend, yrecv.at[back - 2], i, back)]
        return [remote(i, dsend.at[0 if dx < 0 else 1], drecv.at[back - 4], i, back)]

    def send(first, end, p=0):
        for i in range(first, end):
            @pl.when(exists(*sides[i]))
            def _():
                halo_copies(i)[p].start()

    def receive(first, end, p=0):
        for i in range(first, end):
            @pl.when(exists(*sides[i]))
            def _():
                dst = xrecv.at[i, p] if i < 2 else yrecv.at[i - 2] if i < 4 else drecv.at[i - 4]
                remote(i, dst, dst, i + 8 * p, i + 8 * p).wait_recv()

    send(0, 2)
    send(0, 2, 1)
    lane = lax.broadcasted_iota(jnp.int32, (rows, cols), 1)
    row = lax.broadcasted_iota(jnp.int32, (rows, cols), 0)
    slot_lanes = cols // depth
    packs = [zero_tile] * 6
    for z in range(depth):
        window = lax.rem(lane - z * slot_lanes + HALO + cols, cols) < 2 * HALO
        for i, ref in enumerate(targets(z)):
            f = ref[0:rows, 0:cols]
            rolled = pltpu.roll(f, z * slot_lanes, 1) if z else f
            packs[i] = jnp.where(window, rolled, packs[i])
    for i in range(6):
        ysend[i] = packs[i]
    send(2, 4)
    for j in range(2):
        one, other = packs[2 * j], packs[2 * j + 1]
        dsend[0, j] = jnp.where(row < HALO, one, pltpu.roll(other, HALO, 0))
        dsend[1, j] = jnp.where(row >= rows - HALO, one, pltpu.roll(other, rows - HALO, 0))
    send(4, 8)

    receive(2, 4)
    after = lax.rem(lane, slot_lanes) < HALO
    window = jnp.logical_or(lane < HALO, lane >= cols - HALO)
    corner_rows = jnp.logical_or(row < HALO, row >= rows - HALO)
    window_corner = jnp.logical_and(window, corner_rows)

    def unroll_lanes(tile, z):
        back = (cols - z * slot_lanes) % cols
        return pltpu.roll(tile, back, 1) if back else tile

    beside = [jnp.where(after, yrecv[1, i], yrecv[0, i]) for i in range(6)]
    for z in range(depth):
        for f, ref in enumerate(targets(z)):
            ref[0:rows, cols:C2] = jnp.where(window, unroll_lanes(beside[f], z), 0.0)

    receive(4, 8)
    corner = []
    for i in range(4):
        above = jnp.where(after, drecv[1, i // 2], drecv[0, i // 2])
        below = jnp.where(after, drecv[3, i // 2], drecv[2, i // 2])
        if i % 2:
            above = pltpu.roll(above, HALO, 0)
            below = pltpu.roll(below, rows - HALO, 0)
        corner.append(jnp.where(row < rows // 2, below, above))
    for z in range(depth):
        for f, ref in enumerate(targets(z)[:4]):
            ref[rows:R2, cols:C2] = jnp.where(window_corner, unroll_lanes(corner[f], z), 0.0)

    def unpack_x(p):
        for z in range(half):
            at = 0
            for ref, width in zip(targets(p * half + z), (3, 3, 3, 2, 1, 1)):
                first = at + z * width
                ref[rows:rows + width, 0:cols] = xrecv[1, p, first:first + width, :]
                ref[R2 - width:R2, 0:cols] = xrecv[0, p, first:first + width, :]
                at += half * width

    big_row = lax.broadcasted_iota(jnp.int32, (R2, C2), 0)
    big_lane = lax.broadcasted_iota(jnp.int32, (R2, C2), 1)
    no_x = jnp.logical_or(
        jnp.logical_and(big_row == rows - 1, jnp.logical_not(has_down)),
        jnp.logical_and(big_row == R2 - 1, jnp.logical_not(has_up)),
    )
    no_y = jnp.logical_or(
        jnp.logical_and(big_lane == cols - 1, jnp.logical_not(has_right)),
        jnp.logical_and(big_lane == C2 - 1, jnp.logical_not(has_left)),
    )
    valid_x = jnp.where(no_x, 0.0, 1.0)
    valid_y = jnp.where(no_y, 0.0, 1.0)
    half_x = valid_x * (0.5 / SCALE)
    half_y = valid_y * (0.5 / SCALE)
    last = depth - 1

    def next_row(a):
        return pltpu.roll(a, a.shape[0] - 1, 0)

    def next_lane(a):
        return pltpu.roll(a, a.shape[1] - 1, 1)

    def weights(z, carry):
        c = ce[z]
        ex = half_x * (c + next_row(c))
        ey = half_y * (c + next_lane(c))
        cn = ce[jnp.minimum(z + 1, last)]
        ez = jnp.where(z < last, 0.5 / SCALE, 0.0) * (c + cn)
        wx[z] = ex
        wy[z] = ey
        wz[z + 1] = ez
        deg = ex + pltpu.roll(ex, 1, 0) + ey + pltpu.roll(ey, 1, 1) + ez + wz[z]
        dd[z] = deg + (1.0 - SHIFT) / SCALE
        return carry

    def apply_full(src, dst, start, end, sums):
        def body(z, carry):
            ex, ey, ez, ezm, d, m = wx[z], wy[z], wz[z + 1], wz[z], dd[z], me[z]
            out = []
            for k in range(2):
                v = src[k, z + 1]
                a = d * v - ez * src[k, z + 2] - ezm * src[k, z]
                a = a - ex * next_row(v) - pltpu.roll(ex * v, 1, 0)
                a = a - ey * next_lane(v) - pltpu.roll(ey * v, 1, 1)
                a = m * a
                dst[k, z + 1] = a
                old, new = v[0:rows, 0:cols], a[0:rows, 0:cols]
                out.append(carry[3 * k] + old * old)
                out.append(carry[3 * k + 1] + old * new)
                out.append(carry[3 * k + 2] + new * new)
            return tuple(out)
        return lax.fori_loop(start, end, body, sums, unroll=end - start)

    zero_sums = (zero_tile,) * 6
    receive(0, 2)
    unpack_x(0)
    lax.fori_loop(0, half - 1, weights, 0, unroll=half - 1)
    first = apply_full(v0, v1, 0, half - 1, zero_sums)
    receive(0, 2, 1)
    unpack_x(1)
    lax.fori_loop(half - 1, depth, weights, 0, unroll=depth - half + 1)
    first = apply_full(v0, v1, half - 1, depth, first)
    second = apply_full(v1, v2, 0, depth, zero_sums)

    def apply_core(z, carry):
        exr = wx[z, :, 0:cols]
        eyr = wy[z, 0:rows, :]
        ez, ezm = wz[z + 1, 0:rows, 0:cols], wz[z, 0:rows, 0:cols]
        d, m = dd[z, 0:rows, 0:cols], me[z, 0:rows, 0:cols]
        out = []
        for k in range(2):
            vx = v2[k, z + 1, :, 0:cols]
            vy = v2[k, z + 1, 0:rows, :]
            v = vx[0:rows]
            a = d * v - ez * v2[k, z + 2, 0:rows, 0:cols] - ezm * v2[k, z, 0:rows, 0:cols]
            a = a - (exr * next_row(vx) + pltpu.roll(exr * vx, 1, 0))[0:rows]
            a = a - (eyr * next_lane(vy) + pltpu.roll(eyr * vy, 1, 1))[:, 0:cols]
            out.append(carry[k] + v * (m * a))
        return tuple(out)

    third = lax.fori_loop(0, depth, apply_core, (zero_tile,) * 2, unroll=depth)

    for k in range(2):
        moments = [first[3 * k], first[3 * k + 1], first[3 * k + 2],
                   second[3 * k + 1], second[3 * k + 2], third[k]]
        for j, a in enumerate(moments):
            table[8 * k + j:8 * k + j + 1, :] = jnp.sum(a, axis=0, keepdims=True)
        table[8 * k + 6:8 * k + 8, :] = jnp.zeros((2, cols), jnp.float32)
    diagonal = lax.broadcasted_iota(jnp.int32, (16, cols), 0) == lax.broadcasted_iota(jnp.int32, (16, cols), 1)
    sums = jnp.broadcast_to(jnp.sum(table[...], axis=1, keepdims=True), (16, cols))
    pay[...] = jnp.sum(jnp.where(diagonal, sums, 0.0), axis=0, keepdims=True)

    def gx_copy(o):
        return pltpu.make_async_remote_copy(
            src_ref=pay, dst_ref=slots_x.at[gx], send_sem=gx_send.at[o], recv_sem=gx_recv.at[o],
            device_id=(lax.rem(gx + o, n_gx), gy), device_id_type=MESH,
        )

    def gy_copy(o):
        return pltpu.make_async_remote_copy(
            src_ref=mid, dst_ref=slots_y.at[gy], send_sem=gy_send.at[o], recv_sem=gy_recv.at[o],
            device_id=(gx, lax.rem(gy + o, n_gy)), device_id_type=MESH,
        )

    for o in range(1, n_gx):
        gx_copy(o).start()
    slots_x[gx] = pay[...]

    vx_edge = valid_x[:, 0:cols]
    vy_edge = valid_y[0:rows, :]

    def parts(k):
        def body(z, carry):
            up = jnp.minimum(z + 1, last)
            down = jnp.maximum(z - 1, 0)
            px = pe[k, z, :, 0:cols]
            py = pe[k, z, 0:rows, :]
            p = px[0:rows]
            dx = vx_edge * (px - next_row(px))
            dy = vy_edge * (py - next_lane(py))
            du = p - pe[k, up, 0:rows, 0:cols]
            dn = p - pe[k, down, 0:rows, 0:cols]
            for j, v in enumerate((v0, v1, v2)):
                ax = v[k, z + 1, :, 0:cols]
                ay = v[k, z + 1, 0:rows, :]
                a = ax[0:rows]
                qx = dx * (ax - next_row(ax))
                qy = dy * (ay - next_lane(ay))
                g = qx[0:rows] + pltpu.roll(qx, 1, 0)[0:rows]
                g = g + qy[:, 0:cols] + pltpu.roll(qy, 1, 1)[:, 0:cols]
                g = g + du * (a - v[k, z + 2, 0:rows, 0:cols])
                g = g + dn * (a - v[k, z, 0:rows, 0:cols])
                gk[3 * k + j, z] = g
            return carry
        lax.fori_loop(0, depth, body, 0, unroll=depth)

    parts(0)
    for o in range(1, n_gx):
        gx_copy(o).wait_recv()
    total = jnp.sum(slots_x[...], axis=0)
    mid[...] = total
    for o in range(1, n_gy):
        gy_copy(o).start()
    slots_y[gy] = total
    parts(1)
    for o in range(1, n_gy):
        gy_copy(o).wait_recv()
    total = jnp.sum(slots_y[...], axis=0)
    total = jnp.where(diagonal, jnp.broadcast_to(total, (16, cols)), 0.0)
    total = jnp.broadcast_to(jnp.sum(total, axis=1, keepdims=True), (16, cols))

    coeffs = []
    for k in range(2):
        m = [total[8 * k + j:8 * k + j + 1, :] for j in range(6)]
        h = [SCALE * m[j + 1] + SHIFT * m[j] for j in range(5)]
        l1, l2 = h[1] / h[0], h[2] / h[0]
        a11, a12, a22 = h[2] - l1 * h[1], h[3] - l1 * h[2], h[4] - l2 * h[2]
        b1, b2 = m[1] - l1 * m[0], m[2] - l2 * m[0]
        l3 = a12 / a11
        c2 = (b2 - l3 * b1) / (a22 - l3 * a12)
        c1 = (b1 - a12 * c2) / a11
        c0 = (m[0] - h[1] * c1 - h[2] * c2) / h[0]
        coeffs.append([jnp.broadcast_to(c, (rows, cols)) for c in (c0, c1, c2)])

    for z in range(depth):
        grad = zero_tile
        for k in range(2):
            acc = zero_tile
            for j, v in enumerate((v0, v1, v2)):
                acc = acc + coeffs[k][j] * v[k, z + 1, 0:rows, 0:cols]
                grad = grad + coeffs[k][j] * gk[3 * k + j, z]
            adj_ref[k, z] = acc
        grad_ref[z] = -0.5 * grad

    for i, (dx, dy) in enumerate(sides):
        @pl.when(exists(dx, dy))
        def _():
            for copy in halo_copies(i):
                copy.wait_send()
    for o in range(1, n_gx):
        gx_copy(o).wait_send()
    for o in range(1, n_gy):
        gy_copy(o).wait_send()


def write_out(adj_ref, grad_ref, adj_out, grad_out, sem):
    copies = [
        pltpu.make_async_copy(adj_ref, adj_out, sem.at[0]),
        pltpu.make_async_copy(grad_ref, grad_out, sem.at[1]),
    ]
    for copy in copies:
        copy.start()
    for copy in copies:
        copy.wait()


def solution(mesh):
    n_gx, n_gy = mesh.shape["gx"], mesh.shape["gy"]

    def per_device(conductance, labels, cotangent, saved):
        depth, rows, cols = conductance.shape
        f32 = jnp.float32
        big = (depth, 2 * rows, 2 * cols)
        padded = (2, depth + 2, 2 * rows, 2 * cols)
        face = (2, 2, depth // 2 * 13, cols)
        vmem = pl.BlockSpec(memory_space=pltpu.VMEM)
        dma = pltpu.SemaphoreType.DMA
        results = pl.pallas_call(
            lambda *refs: kernel(n_gx, n_gy, *refs),
            out_shape=(
                jax.ShapeDtypeStruct(cotangent.shape, f32),
                jax.ShapeDtypeStruct(conductance.shape, f32),
            ),
            in_specs=[pl.BlockSpec(memory_space=pltpu.HBM)] * 4,
            out_specs=(vmem, vmem),
            scratch_shapes=[
                pltpu.VMEM(conductance.shape, f32),
                pltpu.VMEM(labels.shape, labels.dtype),
                pltpu.VMEM(cotangent.shape, f32),
                pltpu.VMEM(saved.shape, f32),
                dma((4,)),
                pltpu.VMEM(big, f32),
                pltpu.VMEM(big, f32),
                pltpu.VMEM((2,) + big, f32),
                pltpu.VMEM(padded, f32),
                pltpu.VMEM(padded, f32),
                pltpu.VMEM(padded, f32),
                pltpu.VMEM(big, f32),
                pltpu.VMEM(big, f32),
                pltpu.VMEM((depth + 1, 2 * rows, 2 * cols), f32),
                pltpu.VMEM(big, f32),
                pltpu.VMEM((6, depth, rows, cols), f32),
                pltpu.VMEM(face, f32),
                pltpu.VMEM(face, f32),
                pltpu.VMEM((6, rows, cols), f32),
                pltpu.VMEM((2, 6, rows, cols), f32),
                pltpu.VMEM((2, 2, rows, cols), f32),
                pltpu.VMEM((4, 2, rows, cols), f32),
                pltpu.VMEM((16, cols), f32),
                pltpu.VMEM((1, cols), f32),
                pltpu.VMEM((n_gx, 1, cols), f32),
                pltpu.VMEM((1, cols), f32),
                pltpu.VMEM((n_gy, 1, cols), f32),
                dma((10,)),
                dma((10,)),
                dma((n_gx,)),
                dma((n_gx,)),
                dma((n_gy,)),
                dma((n_gy,)),
            ],
            compiler_params=pltpu.CompilerParams(
                collective_id=0, has_side_effects=True, vmem_limit_bytes=63 * 1024 * 1024
            ),
        )(conductance, labels, cotangent, saved)
        hbm = pl.BlockSpec(memory_space=pltpu.HBM)
        return pl.pallas_call(
            write_out,
            out_shape=tuple(jax.ShapeDtypeStruct(r.shape, f32) for r in results),
            in_specs=[hbm] * 2,
            out_specs=(hbm, hbm),
            scratch_shapes=[dma((2,))],
            compiler_params=pltpu.CompilerParams(vmem_limit_bytes=63 * 1024 * 1024),
        )(*results)

    return jax.shard_map(
        per_device,
        mesh=mesh,
        in_specs=(
            P(None, "gx", "gy"),
            P(None, "gx", "gy"),
            P(None, None, "gx", "gy"),
            P(None, None, "gx", "gy"),
        ),
        out_specs=(P(None, None, "gx", "gy"), P(None, "gx", "gy")),
        check_vma=False,
    )
```

```python
import jax
import jax.numpy as jnp
from jax import lax
from jax.experimental import pallas as pl
from jax.experimental.pallas import tpu as pltpu
from jax.sharding import PartitionSpec as P

SHIFT = 2.0
SCALE = 32.0
HALO = 3
MESH = pl.DeviceIdType.MESH


def kernel(
    n_gx, n_gy,
    cond_hbm, label_hbm, cot_hbm, saved_hbm,
    adj_ref, grad_ref,
    cond_ref, label_ref, cot_ref, saved_ref, in_sem,
    ce, me, pe, v0, v1, v2, wx, wy, wz, dd, gk,
    xsend, xrecv, ysend, yrecv, dsend, drecv, table, pay, slots_x, mid, slots_y,
    send_sem, recv_sem, gx_send, gx_recv, gy_send, gy_recv,
):
    depth, rows, cols = cond_ref.shape
    R2, C2 = 2 * rows, 2 * cols
    gx = lax.axis_index("gx")
    gy = lax.axis_index("gy")
    has_up, has_down = gx > 0, gx < n_gx - 1
    has_left, has_right = gy > 0, gy < n_gy - 1

    sides = [(-1, 0), (1, 0), (0, -1), (0, 1), (-1, -1), (-1, 1), (1, -1), (1, 1)]

    def exists(dx, dy):
        ok = None
        for d, low, high in ((dx, has_up, has_down), (dy, has_left, has_right)):
            if d:
                here = low if d < 0 else high
                ok = here if ok is None else jnp.logical_and(ok, here)
        return ok

    fetches = [
        pltpu.make_async_copy(src, dst, in_sem.at[i])
        for i, (src, dst) in enumerate((
            (cond_hbm, cond_ref), (label_hbm, label_ref), (cot_hbm, cot_ref), (saved_hbm, saved_ref),
        ))
    ]
    for fetch in fetches:
        fetch.start()

    barrier = pltpu.get_barrier_semaphore()
    partners = n_gx - 1 + n_gy - 1
    for dx, dy in sides[4:]:
        partners = partners + jnp.where(exists(dx, dy), 1, 0)

        @pl.when(exists(dx, dy))
        def _():
            pl.semaphore_signal(barrier, inc=1, device_id=(gx + dx, gy + dy), device_id_type=MESH)
    for o in range(1, n_gy):
        pl.semaphore_signal(barrier, inc=1, device_id=(gx, lax.rem(gy + o, n_gy)), device_id_type=MESH)
    for o in range(1, n_gx):
        pl.semaphore_signal(barrier, inc=1, device_id=(lax.rem(gx + o, n_gx), gy), device_id_type=MESH)

    zero_tile = jnp.zeros((rows, cols), jnp.float32)

    edge = jnp.zeros((R2, C2), jnp.float32)
    for v in (v0, v1, v2):
        for k in range(2):
            v[k, 0] = edge
            v[k, depth + 1] = edge
    wz[0] = edge
    for z in range(depth):
        for ref in (v0.at[0, z + 1], v0.at[1, z + 1], ce.at[z], me.at[z], pe.at[0, z], pe.at[1, z]):
            ref[rows:R2, 0:cols] = zero_tile
    for i, (dx, dy) in enumerate(sides):
        @pl.when(jnp.logical_not(exists(dx, dy)))
        def _():
            if i < 2:
                xrecv[i] = jnp.zeros(xrecv.shape[1:], jnp.float32)
            elif i < 4:
                yrecv[i - 2] = jnp.zeros(yrecv.shape[1:], jnp.float32)
            else:
                drecv[i - 4] = jnp.zeros(drecv.shape[1:], jnp.float32)

    for fetch in fetches:
        fetch.wait()

    half = depth // 2

    def targets(z):
        return [v0.at[0, z + 1], v0.at[1, z + 1], ce.at[z], me.at[z], pe.at[0, z], pe.at[1, z]]

    for z in range(depth):
        lab = label_ref[z]
        m = jnp.where(lab == 0, 1.0, 0.0)
        fields = [m * cot_ref[0, z], m * cot_ref[1, z], cond_ref[z], m]
        for k in range(2):
            fields.append(jnp.where(lab == k + 1, 1.0, jnp.where(lab > 0, 0.0, saved_ref[k, z])))
        piece, at = z // half, 0
        for f, ref, width in zip(fields, targets(z), (3, 3, 3, 2, 1, 1)):
            ref[0:rows, 0:cols] = f
            first = at + z % half * width
            xsend[0, piece, first:first + width, :] = f[0:width]
            xsend[1, piece, first:first + width, :] = f[rows - width:rows]
            at += half * width

    pl.semaphore_wait(barrier, partners)

    def remote(i, src, dst, send_at, recv_at):
        return pltpu.make_async_remote_copy(
            src_ref=src, dst_ref=dst, send_sem=send_sem.at[send_at], recv_sem=recv_sem.at[recv_at],
            device_id=(gx + sides[i][0], gy + sides[i][1]), device_id_type=MESH,
        )

    def halo_copies(i):
        dx, dy = sides[i]
        back = sides.index((-dx, -dy))
        if dy == 0:
            return [
                remote(i, xsend.at[i, p], xrecv.at[back, p], i + 8 * p, back + 8 * p) for p in range(2)
            ]
        if dx == 0:
            return [remote(i, ysend, yrecv.at[back - 2], i, back)]
        return [remote(i, dsend.at[0 if dx < 0 else 1], drecv.at[back - 4], i, back)]

    def send(first, end, p=0):
        for i in range(first, end):
            @pl.when(exists(*sides[i]))
            def _():
                halo_copies(i)[p].start()

    def receive(first, end, p=0):
        for i in range(first, end):
            @pl.when(exists(*sides[i]))
            def _():
                dst = xrecv.at[i, p] if i < 2 else yrecv.at[i - 2] if i < 4 else drecv.at[i - 4]
                remote(i, dst, dst, i + 8 * p, i + 8 * p).wait_recv()

    send(0, 2)
    send(0, 2, 1)
    lane = lax.broadcasted_iota(jnp.int32, (rows, cols), 1)
    row = lax.broadcasted_iota(jnp.int32, (rows, cols), 0)
    slot_lanes = cols // depth
    packs = [zero_tile] * 6
    for z in range(depth):
        window = lax.rem(lane - z * slot_lanes + HALO + cols, cols) < 2 * HALO
        for i, ref in enumerate(targets(z)):
            f = ref[0:rows, 0:cols]
            rolled = pltpu.roll(f, z * slot_lanes, 1) if z else f
            packs[i] = jnp.where(window, rolled, packs[i])
    for i in range(6):
        ysend[i] = packs[i]
    send(2, 4)
    for j in range(2):
        one, other = packs[2 * j], packs[2 * j + 1]
        dsend[0, j] = jnp.where(row < HALO, one, pltpu.roll(other, HALO, 0))
        dsend[1, j] = jnp.where(row >= rows - HALO, one, pltpu.roll(other, rows - HALO, 0))
    send(4, 8)

    receive(2, 4)
    after = lax.rem(lane, slot_lanes) < HALO
    window = jnp.logical_or(lane < HALO, lane >= cols - HALO)
    corner_rows = jnp.logical_or(row < HALO, row >= rows - HALO)
    window_corner = jnp.logical_and(window, corner_rows)

    def unroll_lanes(tile, z):
        back = (cols - z * slot_lanes) % cols
        return pltpu.roll(tile, back, 1) if back else tile

    beside = [jnp.where(after, yrecv[1, i], yrecv[0, i]) for i in range(6)]
    for z in range(depth):
        for f, ref in enumerate(targets(z)):
            ref[0:rows, cols:C2] = jnp.where(window, unroll_lanes(beside[f], z), 0.0)

    receive(4, 8)
    corner = []
    for i in range(4):
        above = jnp.where(after, drecv[1, i // 2], drecv[0, i // 2])
        below = jnp.where(after, drecv[3, i // 2], drecv[2, i // 2])
        if i % 2:
            above = pltpu.roll(above, HALO, 0)
            below = pltpu.roll(below, rows - HALO, 0)
        corner.append(jnp.where(row < rows // 2, below, above))
    for z in range(depth):
        for f, ref in enumerate(targets(z)[:4]):
            ref[rows:R2, cols:C2] = jnp.where(window_corner, unroll_lanes(corner[f], z), 0.0)

    def unpack_x(p):
        for z in range(half):
            at = 0
            for ref, width in zip(targets(p * half + z), (3, 3, 3, 2, 1, 1)):
                first = at + z * width
                ref[rows:rows + width, 0:cols] = xrecv[1, p, first:first + width, :]
                ref[R2 - width:R2, 0:cols] = xrecv[0, p, first:first + width, :]
                at += half * width

    big_row = lax.broadcasted_iota(jnp.int32, (R2, C2), 0)
    big_lane = lax.broadcasted_iota(jnp.int32, (R2, C2), 1)
    no_x = jnp.logical_or(
        jnp.logical_and(big_row == rows - 1, jnp.logical_not(has_down)),
        jnp.logical_and(big_row == R2 - 1, jnp.logical_not(has_up)),
    )
    no_y = jnp.logical_or(
        jnp.logical_and(big_lane == cols - 1, jnp.logical_not(has_right)),
        jnp.logical_and(big_lane == C2 - 1, jnp.logical_not(has_left)),
    )
    valid_x = jnp.where(no_x, 0.0, 1.0)
    valid_y = jnp.where(no_y, 0.0, 1.0)
    half_x = valid_x * (0.5 / SCALE)
    half_y = valid_y * (0.5 / SCALE)
    last = depth - 1

    def next_row(a):
        return pltpu.roll(a, a.shape[0] - 1, 0)

    def next_lane(a):
        return pltpu.roll(a, a.shape[1] - 1, 1)

    def weights(z, carry):
        c = ce[z]
        ex = half_x * (c + next_row(c))
        ey = half_y * (c + next_lane(c))
        cn = ce[jnp.minimum(z + 1, last)]
        ez = jnp.where(z < last, 0.5 / SCALE, 0.0) * (c + cn)
        wx[z] = ex
        wy[z] = ey
        wz[z + 1] = ez
        deg = ex + pltpu.roll(ex, 1, 0) + ey + pltpu.roll(ey, 1, 1) + ez + wz[z]
        dd[z] = deg + (1.0 - SHIFT) / SCALE
        return carry

    def apply_full(src, dst, start, end, sums):
        def body(z, carry):
            ex, ey, ez, ezm, d, m = wx[z], wy[z], wz[z + 1], wz[z], dd[z], me[z]
            out = []
            for k in range(2):
                v = src[k, z + 1]
                a = d * v - ez * src[k, z + 2] - ezm * src[k, z]
                a = a - ex * next_row(v) - pltpu.roll(ex * v, 1, 0)
                a = a - ey * next_lane(v) - pltpu.roll(ey * v, 1, 1)
                a = m * a
                dst[k, z + 1] = a
                old, new = v[0:rows, 0:cols], a[0:rows, 0:cols]
                out.append(carry[3 * k] + old * old)
                out.append(carry[3 * k + 1] + old * new)
                out.append(carry[3 * k + 2] + new * new)
            return tuple(out)
        return lax.fori_loop(start, end, body, sums, unroll=end - start)

    zero_sums = (zero_tile,) * 6
    receive(0, 2)
    unpack_x(0)
    lax.fori_loop(0, half - 1, weights, 0, unroll=half - 1)
    first = apply_full(v0, v1, 0, half - 1, zero_sums)
    receive(0, 2, 1)
    unpack_x(1)
    lax.fori_loop(half - 1, depth, weights, 0, unroll=depth - half + 1)
    first = apply_full(v0, v1, half - 1, depth, first)
    second = apply_full(v1, v2, 0, depth, zero_sums)

    def apply_core(z, carry):
        exr = wx[z, :, 0:cols]
        eyr = wy[z, 0:rows, :]
        ez, ezm = wz[z + 1, 0:rows, 0:cols], wz[z, 0:rows, 0:cols]
        d, m = dd[z, 0:rows, 0:cols], me[z, 0:rows, 0:cols]
        out = []
        for k in range(2):
            vx = v2[k, z + 1, :, 0:cols]
            vy = v2[k, z + 1, 0:rows, :]
            v = vx[0:rows]
            a = d * v - ez * v2[k, z + 2, 0:rows, 0:cols] - ezm * v2[k, z, 0:rows, 0:cols]
            a = a - (exr * next_row(vx) + pltpu.roll(exr * vx, 1, 0))[0:rows]
            a = a - (eyr * next_lane(vy) + pltpu.roll(eyr * vy, 1, 1))[:, 0:cols]
            out.append(carry[k] + v * (m * a))
        return tuple(out)

    third = lax.fori_loop(0, depth, apply_core, (zero_tile,) * 2, unroll=depth)

    for k in range(2):
        moments = [first[3 * k], first[3 * k + 1], first[3 * k + 2],
                   second[3 * k + 1], second[3 * k + 2], third[k]]
        for j, a in enumerate(moments):
            table[8 * k + j:8 * k + j + 1, :] = jnp.sum(a, axis=0, keepdims=True)
        table[8 * k + 6:8 * k + 8, :] = jnp.zeros((2, cols), jnp.float32)
    diagonal = lax.broadcasted_iota(jnp.int32, (16, cols), 0) == lax.broadcasted_iota(jnp.int32, (16, cols), 1)
    sums = jnp.broadcast_to(jnp.sum(table[...], axis=1, keepdims=True), (16, cols))
    pay[...] = jnp.sum(jnp.where(diagonal, sums, 0.0), axis=0, keepdims=True)

    def gx_copy(o):
        return pltpu.make_async_remote_copy(
            src_ref=pay, dst_ref=slots_x.at[gx], send_sem=gx_send.at[o], recv_sem=gx_recv.at[o],
            device_id=(lax.rem(gx + o, n_gx), gy), device_id_type=MESH,
        )

    def gy_copy(o):
        return pltpu.make_async_remote_copy(
            src_ref=mid, dst_ref=slots_y.at[gy], send_sem=gy_send.at[o], recv_sem=gy_recv.at[o],
            device_id=(gx, lax.rem(gy + o, n_gy)), device_id_type=MESH,
        )

    for o in range(1, n_gx):
        gx_copy(o).start()
    slots_x[gx] = pay[...]

    vx_edge = valid_x[:, 0:cols]
    vy_edge = valid_y[0:rows, :]

    def parts(k):
        def body(z, carry):
            up = jnp.minimum(z + 1, last)
            down = jnp.maximum(z - 1, 0)
            px = pe[k, z, :, 0:cols]
            py = pe[k, z, 0:rows, :]
            p = px[0:rows]
            dx = vx_edge * (px - next_row(px))
            dy = vy_edge * (py - next_lane(py))
            du = p - pe[k, up, 0:rows, 0:cols]
            dn = p - pe[k, down, 0:rows, 0:cols]
            for j, v in enumerate((v0, v1, v2)):
                ax = v[k, z + 1, :, 0:cols]
                ay = v[k, z + 1, 0:rows, :]
                a = ax[0:rows]
                qx = dx * (ax - next_row(ax))
                qy = dy * (ay - next_lane(ay))
                g = qx[0:rows] + pltpu.roll(qx, 1, 0)[0:rows]
                g = g + qy[:, 0:cols] + pltpu.roll(qy, 1, 1)[:, 0:cols]
                g = g + du * (a - v[k, z + 2, 0:rows, 0:cols])
                g = g + dn * (a - v[k, z, 0:rows, 0:cols])
                gk[3 * k + j, z] = g
            return carry
        lax.fori_loop(0, depth, body, 0, unroll=depth)

    parts(0)
    for o in range(1, n_gx):
        gx_copy(o).wait_recv()
    total = jnp.sum(slots_x[...], axis=0)
    mid[...] = total
    for o in range(1, n_gy):
        gy_copy(o).start()
    slots_y[gy] = total
    parts(1)
    for o in range(1, n_gy):
        gy_copy(o).wait_recv()
    total = jnp.sum(slots_y[...], axis=0)
    total = jnp.where(diagonal, jnp.broadcast_to(total, (16, cols)), 0.0)
    total = jnp.broadcast_to(jnp.sum(total, axis=1, keepdims=True), (16, cols))

    coeffs = []
    for k in range(2):
        m = [total[8 * k + j:8 * k + j + 1, :] for j in range(6)]
        h = [SCALE * m[j + 1] + SHIFT * m[j] for j in range(5)]
        l1, l2 = h[1] / h[0], h[2] / h[0]
        a11, a12, a22 = h[2] - l1 * h[1], h[3] - l1 * h[2], h[4] - l2 * h[2]
        b1, b2 = m[1] - l1 * m[0], m[2] - l2 * m[0]
        l3 = a12 / a11
        c2 = (b2 - l3 * b1) / (a22 - l3 * a12)
        c1 = (b1 - a12 * c2) / a11
        c0 = (m[0] - h[1] * c1 - h[2] * c2) / h[0]
        coeffs.append([jnp.broadcast_to(c, (rows, cols)) for c in (c0, c1, c2)])

    for z in range(depth):
        grad = zero_tile
        for k in range(2):
            acc = zero_tile
            for j, v in enumerate((v0, v1, v2)):
                acc = acc + coeffs[k][j] * v[k, z + 1, 0:rows, 0:cols]
                grad = grad + coeffs[k][j] * gk[3 * k + j, z]
            adj_ref[k, z] = acc
        grad_ref[z] = -0.5 * grad

    for i, (dx, dy) in enumerate(sides):
        @pl.when(exists(dx, dy))
        def _():
            for copy in halo_copies(i):
                copy.wait_send()
    for o in range(1, n_gx):
        gx_copy(o).wait_send()
    for o in range(1, n_gy):
        gy_copy(o).wait_send()


def solution(mesh):
    n_gx, n_gy = mesh.shape["gx"], mesh.shape["gy"]

    def per_device(conductance, labels, cotangent, saved):
        depth, rows, cols = conductance.shape
        f32 = jnp.float32
        big = (depth, 2 * rows, 2 * cols)
        padded = (2, depth + 2, 2 * rows, 2 * cols)
        face = (2, 2, depth // 2 * 13, cols)
        vmem = pl.BlockSpec(memory_space=pltpu.VMEM)
        dma = pltpu.SemaphoreType.DMA
        return pl.pallas_call(
            lambda *refs: kernel(n_gx, n_gy, *refs),
            out_shape=(
                jax.ShapeDtypeStruct(cotangent.shape, f32),
                jax.ShapeDtypeStruct(conductance.shape, f32),
            ),
            in_specs=[pl.BlockSpec(memory_space=pltpu.HBM)] * 4,
            out_specs=(vmem, vmem),
            scratch_shapes=[
                pltpu.VMEM(conductance.shape, f32),
                pltpu.VMEM(labels.shape, labels.dtype),
                pltpu.VMEM(cotangent.shape, f32),
                pltpu.VMEM(saved.shape, f32),
                dma((4,)),
                pltpu.VMEM(big, f32),
                pltpu.VMEM(big, f32),
                pltpu.VMEM((2,) + big, f32),
                pltpu.VMEM(padded, f32),
                pltpu.VMEM(padded, f32),
                pltpu.VMEM(padded, f32),
                pltpu.VMEM(big, f32),
                pltpu.VMEM(big, f32),
                pltpu.VMEM((depth + 1, 2 * rows, 2 * cols), f32),
                pltpu.VMEM(big, f32),
                pltpu.VMEM((6, depth, rows, cols), f32),
                pltpu.VMEM(face, f32),
                pltpu.VMEM(face, f32),
                pltpu.VMEM((6, rows, cols), f32),
                pltpu.VMEM((2, 6, rows, cols), f32),
                pltpu.VMEM((2, 2, rows, cols), f32),
                pltpu.VMEM((4, 2, rows, cols), f32),
                pltpu.VMEM((16, cols), f32),
                pltpu.VMEM((1, cols), f32),
                pltpu.VMEM((n_gx, 1, cols), f32),
                pltpu.VMEM((1, cols), f32),
                pltpu.VMEM((n_gy, 1, cols), f32),
                dma((10,)),
                dma((10,)),
                dma((n_gx,)),
                dma((n_gx,)),
                dma((n_gy,)),
                dma((n_gy,)),
            ],
            compiler_params=pltpu.CompilerParams(
                collective_id=0, has_side_effects=True, vmem_limit_bytes=63 * 1024 * 1024
            ),
        )(conductance, labels, cotangent, saved)

    return jax.shard_map(
        per_device,
        mesh=mesh,
        in_specs=(
            P(None, "gx", "gy"),
            P(None, "gx", "gy"),
            P(None, None, "gx", "gy"),
            P(None, None, "gx", "gy"),
        ),
        out_specs=(P(None, None, "gx", "gy"), P(None, "gx", "gy")),
        check_vma=False,
    )
```
